256 devices in a mesh: scene: 2 (over core), ctx: 16 (over y, x), tp: 8 (over z).
Axes of the slice: x: 4, y: 4, z: 8, core: 2. Of those that a mesh axis runs over, the one named last changes fastest.
Arguments:
- queries: bfloat16 [4096, 8192], P(('scene', 'ctx'), 'tp'), parts along dimension 0, may hold values from -6 to 6
- prefix_keys: bfloat16 [32768, 1024], P(('scene', 'ctx'), 'tp'), parts along dimension 0, may hold values from -8 to 8
- scene_prefix_values: bfloat16 [32768, 1024], P(('scene', 'ctx'), 'tp'), parts along dimension 0, may hold values from -48 to 48
- question_token_keys: bfloat16 [4096, 1024], P(('scene', 'ctx'), 'tp'), parts along dimension 0, may hold values from -12 to 12
- question_token_values: bfloat16 [4096, 1024], P(('scene', 'ctx'), 'tp'), parts along dimension 0, may hold values from -48 to 48
- lengths: int32 [32], P(('scene', 'ctx')), parts along dimension 0, may hold values from 1 to 128, 1280 in all
Outputs:
- attention: bfloat16 [4096, 8192], P(('scene', 'ctx'), 'tp'), parts along dimension 0
The draws below stay inside these ranges and needn't reach their ends.
There are 2 independent parts, one for each index of `scene`. The reference program is written for one: setup_inputs(seed, part) draws one part's arguments, and reference() takes and returns one part's arrays. A program takes and returns all parts, laid end to end along the dimension named above; each array names one. Nothing has to cross between parts.
Inputs may be any that keep to these rules, and one draw needn't show every extreme that they name: Each span holds at least one question token, and some span is full with 128; the sum is taken per scene: the 16 lengths of one scene add up to 1280, so the whole array over all scenes sums to that times the number of scenes.
All inputs are finite; a program needn't handle non-finite values. No bound on the sum of `lengths` on one device may be relied on, other than what follows from the above.
Results may differ from the reference program's by a relative error of at most 0.015.
Values may be sent and summed in bfloat16 or wider, within the bound.
A program may use at most 64 MiB of HBM per device.

```python
import math
import jax
import jax.numpy as jnp
import numpy as np
from jax import lax

QUERY_HEADS = 64
KEY_VALUE_HEADS = 8
HEAD_WIDTH = 128
SPAN = 128
PREFIX_TOKENS = 16384
NCH = 16
QUESTION_SLOTS = 2048


def draw_queries(key, part):
    key = jax.random.fold_in(key, 1)
    sampled_draw = jnp.clip(jax.random.normal(key, (QUESTION_SLOTS, QUERY_HEADS * HEAD_WIDTH), jnp.float32), -5.5, 5.5)
    return sampled_draw.astype(jnp.bfloat16)


def draw_prefix_keys(key, part):
    key = jax.random.fold_in(key, 2)
    sampled_draw = 2.0 * jnp.clip(jax.random.normal(key, (PREFIX_TOKENS, KEY_VALUE_HEADS * HEAD_WIDTH), jnp.float32), -4.0, 4.0)
    return sampled_draw.astype(jnp.bfloat16)


def shard_levels(stream_key, shape, split, smallest, top_value):
    def one(axis_at, shards_of):
        draws = jax.random.uniform(jax.random.fold_in(jax.random.fold_in(stream_key, 6), axis_at), (shards_of,), jnp.float32, smallest / len(split), top_value / len(split))
        return jnp.repeat(jnp.exp(draws), shape[axis_at] // shards_of).reshape((-1,) + (1,) * (len(shape) - axis_at - 1))

    level = one(*split[0])
    for cut in split[1:]:
        level = level * one(*cut)
    return level


def length_profile(amount, total, limit, skew):
    loads = [(1 << 20) // math.isqrt(standing ** skew) + 1 for standing in range(2, amount + 1)]
    rest, holding = total - limit - (amount - 1), [1] * (amount - 1)
    while rest > 0:
        movable = [i for i in range(amount - 1) if holding[i] < limit]
        pool, left = sum([loads[i] for i in movable]), rest
        for i in movable:
            addition = min(limit - holding[i], max(1, left * loads[i] // pool), rest)
            holding[i] = holding[i] + addition
            rest = rest - addition
    return np.array([limit] + holding)


def uneven(own_key, number_of, total, reach, slope):
    if number_of == 2:
        one = jax.random.randint(own_key, (), max(1, total - reach), min(reach, total - 1) + 1)
        return jnp.stack([one, total - one])
    sizes = jnp.asarray(length_profile(number_of, total, reach, slope), jnp.int32)
    couples = (number_of - 1) // 2
    giver, taker = sizes[1:1 + 2 * couples:2], sizes[2:2 + 2 * couples:2]
    slack = jnp.minimum(giver - 1, reach - taker)
    passed = jax.random.randint(jax.random.fold_in(own_key, 1), (couples,), 0, 1 << 20) % (slack + 1)
    sizes = sizes.at[1:1 + 2 * couples:2].set(giver - passed).at[2:2 + 2 * couples:2].set(taker + passed)
    return sizes[jax.random.permutation(jax.random.fold_in(own_key, 2), number_of)]


def bell_draw(stream_key, extent, spread, reach, shards=(), kind=jnp.bfloat16):
    array = spread * jax.random.normal(stream_key, extent, jnp.float32)
    if shards:
        array = array * shard_levels(stream_key, extent, shards, -0.22, 0.18)
    return jnp.clip(array, -reach, reach).astype(kind)


def setup_inputs(seed: int = 0, part: int = 0) -> dict:
    arg_keys = jax.random.split(jax.random.key(seed), 7)
    part_splits = jax.random.split(jax.random.fold_in(arg_keys[6], part), 7)
    return {
        "queries": draw_queries(jax.random.fold_in(jax.random.fold_in(arg_keys[6], part), 71), part),
        "prefix_keys": draw_prefix_keys(jax.random.fold_in(jax.random.fold_in(arg_keys[6], part), 71), part),
        "scene_prefix_values": bell_draw(part_splits[2], (PREFIX_TOKENS, KEY_VALUE_HEADS * HEAD_WIDTH), 8.0, 48.0, ((0, 16), (1, 8))),
        "question_token_keys": bell_draw(part_splits[3], (QUESTION_SLOTS, KEY_VALUE_HEADS * HEAD_WIDTH), 3.0, 12.0, ((0, 16), (1, 8))),
        "question_token_values": bell_draw(part_splits[4], (QUESTION_SLOTS, KEY_VALUE_HEADS * HEAD_WIDTH), 8.0, 48.0, ((0, 16), (1, 8))),
        "lengths": uneven(part_splits[5], NCH, 5 * NCH * SPAN // 8, SPAN, 1).astype(jnp.int32),
    }


def reference(queries, prefix_keys, scene_prefix_values, question_token_keys, question_token_values, lengths):
    queries_per_group = QUERY_HEADS // KEY_VALUE_HEADS
    score_scale = 1.0 / math.sqrt(HEAD_WIDTH)
    token = jnp.arange(QUESTION_SLOTS, dtype=jnp.int32)
    span_index = token // SPAN
    position = token % SPAN
    span_length = lengths[span_index]
    live_rows = position < span_length
    visible = (span_index[:, None] == span_index[None, :]) & (position[None, :] <= position[:, None]) & (position[None, :] < span_length[:, None])

    def one_head(head_index):
        kv_index = (head_index // queries_per_group).astype(jnp.int32)
        query_block = lax.dynamic_slice_in_dim(queries, (head_index * HEAD_WIDTH).astype(jnp.int32), HEAD_WIDTH, 1)
        key_block = lax.dynamic_slice_in_dim(prefix_keys, (kv_index * HEAD_WIDTH).astype(jnp.int32), HEAD_WIDTH, 1)
        value_block = lax.dynamic_slice_in_dim(scene_prefix_values, (kv_index * HEAD_WIDTH).astype(jnp.int32), HEAD_WIDTH, 1)
        own_keys = lax.dynamic_slice_in_dim(question_token_keys, (kv_index * HEAD_WIDTH).astype(jnp.int32), HEAD_WIDTH, 1)
        own_values = lax.dynamic_slice_in_dim(question_token_values, (kv_index * HEAD_WIDTH).astype(jnp.int32), HEAD_WIDTH, 1)
        prefix_scores = jnp.dot(query_block, key_block.T, preferred_element_type=jnp.float32) * score_scale
        own_scores = jnp.dot(query_block, own_keys.T, preferred_element_type=jnp.float32) * score_scale
        own_scores = jnp.where(visible, own_scores, -jnp.inf)
        row_peak = jnp.maximum(lax.optimization_barrier(jnp.max(prefix_scores, axis=1)), lax.optimization_barrier(jnp.max(own_scores, axis=1)))
        prefix_weights = jnp.exp(prefix_scores - row_peak[:, None])
        own_weights = jnp.exp(own_scores - row_peak[:, None])
        row_total = lax.optimization_barrier(jnp.sum(prefix_weights, axis=1)) + lax.optimization_barrier(jnp.sum(own_weights, axis=1))
        summed = jnp.dot(prefix_weights.astype(jnp.bfloat16), value_block, preferred_element_type=jnp.float32)
        summed = summed + jnp.dot(own_weights.astype(jnp.bfloat16), own_values, preferred_element_type=jnp.float32)
        return summed / row_total[:, None]
    heads = lax.map(one_head, jnp.arange(QUERY_HEADS, dtype=jnp.int32))
    result = jnp.transpose(heads, (1, 0, 2)).reshape(QUESTION_SLOTS, QUERY_HEADS * HEAD_WIDTH)
    return jnp.where(live_rows[:, None], result, 0.0).astype(jnp.bfloat16)
```

```python
import functools
import math

import jax
import jax.numpy as jnp
from jax import lax
from jax.experimental import pallas as pl
from jax.experimental.pallas import tpu as pltpu
from jax.sharding import PartitionSpec as P

MESH = pl.DeviceIdType.MESH
F32, BF16 = jnp.float32, jnp.bfloat16
D = 128
H = 8
T = 128
ROWS = 1024
HALF = 512
SIDE = 4
EXTRA = 16
SCALE = math.log2(math.e) / math.sqrt(D)


def block_of(i):
    inner = lax.div(i + 15, 16)
    tail = lax.div(i, 13)
    pair = lax.div(i + 2, 3) - 1
    place = lax.rem(i + 2, 3)
    slot = 1 + place + lax.div(pair + 1, 4) * (2 - 2 * place)
    middle = inner * (1 - tail)
    return middle * slot, middle * pair + tail * (i - 12)


def kernel(q_in, k_in, v_in, ok_in, ov_in, len_ref, out_ref,
           q, kv, acc, mx, sm, s0, s1, x0, x1,
           o_send, st_send, f_recv, fst_recv, o_recv, ost_recv,
           q_ssem, q_rsem, kv_ssem, kv_rsem, o_ssem, o_rsem, st_ssem, st_rsem):
    me = lax.axis_index("ctx")
    y, x = lax.div(me, SIDE), lax.rem(me, SIDE)
    right = y * SIDE + lax.rem(x + 1, SIDE)
    left = y * SIDE + lax.rem(x + SIDE - 1, SIDE)
    up = lax.rem(y + 1, SIDE) * SIDE + x
    down = lax.rem(y + SIDE - 1, SIDE) * SIDE + x

    barrier = pltpu.get_barrier_semaphore()
    for other in (left, right, up, down):
        pl.semaphore_signal(barrier, inc=1, device_id={"ctx": other}, device_id_type=MESH)

    def remote(src, dst, ssem, rsem, to):
        return pltpu.make_async_remote_copy(
            src_ref=src, dst_ref=dst, send_sem=ssem, recv_sem=rsem,
            device_id={"ctx": to}, device_id_type=MESH)

    def q_copy(n):
        src, half, dst, to = ((0, 0, 1, right), (0, 1, 2, left), (0, 1, 1, right), (0, 0, 2, left),
                              (1, 0, 3, right), (2, 1, 3, left))[n]
        return remote(q.at[src, half], q.at[dst, half], q_ssem.at[n], q_rsem.at[n], to)

    def kv_copy(n):
        src, dst, to = ((0, 2, up), (1, 3, down), (1, 4, up), (0, 5, down), (2, 6, up), (3, 7, down))[n]
        return remote(kv.at[src], kv.at[dst], kv_ssem.at[n], kv_rsem.at[n], to)

    def o_copy(n):
        to = (right, left, right, right, left, left)[n]
        if n < 2:
            od, sd = f_recv.at[n], fst_recv.at[n]
        else:
            od, sd = o_recv.at[n - 2], ost_recv.at[n - 2]
        return (remote(o_send.at[n], od, o_ssem.at[n], o_rsem.at[n], to),
                remote(st_send.at[n], sd, st_ssem.at[n], st_rsem.at[n], to))

    def start_o(n):
        for c in o_copy(n):
            c.start()

    def wait_o(n):
        for c in o_copy(n):
            c.wait_recv()

    def transposed(a):
        return a.astype(F32).T.astype(BF16)

    for h in range(H):
        q[0, h // 4, :, (h % 4) * T:(h % 4 + 1) * T] = transposed(q_in[:, h * D:(h + 1) * D])
    pl.semaphore_wait(barrier, 4)
    for n in range(4):
        q_copy(n).start()
    for c in range(2):
        kv[c, 0:HALF, :] = k_in[c * HALF:(c + 1) * HALF, :]
        for b in range(HALF // 128):
            lo = c * HALF + b * 128
            kv[c, HALF + b * 128:HALF + (b + 1) * 128, :] = transposed(v_in[lo:lo + 128, :])
    for n in range(4):
        kv_copy(n).start()

    def values_of(ref_blocks):
        vt = jnp.concatenate(ref_blocks, axis=1)
        return jnp.concatenate([vt, jnp.ones((EXTRA, vt.shape[1]), BF16)], axis=0)

    length = len_ref[0]
    own_v = values_of([transposed(ov_in[...])])
    key_at = lax.broadcasted_iota(jnp.int32, (T, HALF), 0)
    token = lax.rem(lax.broadcasted_iota(jnp.int32, (T, HALF), 1), T)
    visible = (key_at <= token) & (key_at < length)
    for u in range(2):
        s = jnp.dot(ok_in[...], q[0, u], preferred_element_type=F32)
        s = jnp.where(visible, s, -1e30)
        m = jnp.max(s, axis=0, keepdims=True)
        p = jnp.exp2(s * SCALE - m * SCALE)
        d = jnp.dot(own_v, p.astype(BF16), preferred_element_type=F32)
        acc[0, u] = d[:D]
        mx[0, u, 0:1] = m
        sm[0, u, 0:1] = d[D:D + 1]
        for s in range(1, 4):
            acc[s, u] = jnp.zeros((D, HALF), F32)
            mx[s, u, 0:1] = jnp.full((1, HALF), -1e30, F32)
            sm[s, u, 0:1] = jnp.zeros((1, HALF), F32)

    def scores(slot, chunk, u, s_ref, x_ref):
        s = jnp.dot(kv[chunk, 0:HALF, :], q[slot, u], preferred_element_type=F32)
        s_ref[u] = s
        x_ref[u] = jnp.broadcast_to(jnp.max(s, axis=0, keepdims=True), (8, HALF))

    def absorb(slot, chunk, u, s_ref, x_ref):
        vt = values_of([kv[chunk, HALF + b * 128:HALF + (b + 1) * 128, :] for b in range(HALF // 128)])
        m, l = mx[slot, u, 0:1], sm[slot, u, 0:1]
        new = jnp.maximum(m, x_ref[u, 0:1])
        p = jnp.exp2(s_ref[u] * SCALE - new * SCALE)
        a = jnp.exp2((m - new) * SCALE)
        d = jnp.dot(vt, p.astype(BF16), preferred_element_type=F32)
        sm[slot, u, 0:1] = l * a + d[D:D + 1]
        acc[slot, u] = acc[slot, u] * a + d[:D]
        mx[slot, u, 0:1] = new

    def block(i, last=False):
        slot, pair = block_of(i)
        for u in range(2):
            scores(slot, 2 * pair + 1, u, s1, x1)
            absorb(slot, 2 * pair, u, s0, x0)
        if not last:
            slot2, pair2 = block_of(i + 1)
        for u in range(2):
            if not last:
                scores(slot2, 2 * pair2, u, s0, x0)
            absorb(slot, 2 * pair + 1, u, s1, x1)

    def pack(n, slot, u):
        o_send[n] = acc[slot, u].astype(BF16)
        st_send[n, 0:1] = mx[slot, u, 0:1]
        st_send[n, 1:2] = sm[slot, u, 0:1]

    def merge(slot, u, o_ref, st_ref):
        m, l = mx[slot, u, 0:1], sm[slot, u, 0:1]
        m2, l2 = st_ref[0:1], st_ref[1:2]
        new = jnp.maximum(m, m2)
        a, a2 = jnp.exp2((m - new) * SCALE), jnp.exp2((m2 - new) * SCALE)
        acc[slot, u] = acc[slot, u] * a + o_ref[...].astype(F32) * a2
        sm[slot, u, 0:1] = l * a + l2 * a2
        mx[slot, u, 0:1] = new

    for u in range(2):
        scores(0, 0, u, s0, x0)

    def body(i, carry):
        @pl.when(i == 0)
        def _():
            q_copy(0).wait_recv()
            q_copy(4).start()
            q_copy(1).wait_recv()
            q_copy(5).start()
            q_copy(2).wait_recv()

        @pl.when(i == 1)
        def _():
            q_copy(3).wait_recv()

        @pl.when(i == 2)
        def _():
            q_copy(4).wait_recv()
            q_copy(5).wait_recv()

        @pl.when(i == 3)
        def _():
            kv_copy(0).wait_recv()
            kv_copy(4).start()
            kv_copy(1).wait_recv()
            kv_copy(5).start()

        @pl.when(i == 6)
        def _():
            kv_copy(2).wait_recv()
            kv_copy(3).wait_recv()

        @pl.when(i == 9)
        def _():
            kv_copy(4).wait_recv()
            kv_copy(5).wait_recv()

        @pl.when(i == 11)
        def _():
            for u in range(2):
                pack(u, 3, u)
                start_o(u)

        @pl.when(i == 12)
        def _():
            pack(2, 2, 1)
            start_o(2)

        @pl.when(i == 13)
        def _():
            pack(4, 1, 0)
            start_o(4)

        @pl.when(i == 14)
        def _():
            wait_o(0)
            merge(2, 0, f_recv.at[0], fst_recv.at[0])
            pack(3, 2, 0)
            start_o(3)
            wait_o(1)
            merge(1, 1, f_recv.at[1], fst_recv.at[1])
            pack(5, 1, 1)
            start_o(5)

        block(i)
        return carry

    lax.fori_loop(0, 15, body, 0)
    block(15, last=True)

    rows = lax.broadcasted_iota(jnp.int32, (T, D), 0)
    for u, a, b in ((0, 3, 4), (1, 2, 5)):
        for n in (a, b):
            wait_o(n)
            merge(0, u, o_recv.at[n - 2], ost_recv.at[n - 2])
        result = acc[0, u] / sm[0, u, 0:1]
        for h in range(4):
            piece = result[:, h * T:(h + 1) * T].T
            at = (u * 4 + h) * D
            out_ref[:, at:at + D] = jnp.where(rows < length, piece, 0.0).astype(BF16)

    for n in range(6):
        q_copy(n).wait_send()
        kv_copy(n).wait_send()
        for c in o_copy(n):
            c.wait_send()


def shards(queries, prefix_keys, prefix_values, own_keys, own_values, lengths):
    vmem = pl.BlockSpec(memory_space=pltpu.VMEM)
    dma = pltpu.SemaphoreType.DMA
    return pl.pallas_call(
        kernel,
        out_shape=jax.ShapeDtypeStruct((T, H * D), BF16),
        in_specs=[vmem] * 5 + [pl.BlockSpec(memory_space=pltpu.SMEM)],
        out_specs=vmem,
        scratch_shapes=[
            pltpu.VMEM((4, 2, D, HALF), BF16),
            pltpu.VMEM((8, 2 * HALF, D), BF16),
            pltpu.VMEM((4, 2, D, HALF), F32),
            pltpu.VMEM((4, 2, 8, HALF), F32),
            pltpu.VMEM((4, 2, 8, HALF), F32),
            pltpu.VMEM((2, HALF, HALF), F32),
            pltpu.VMEM((2, HALF, HALF), F32),
            pltpu.VMEM((2, 8, HALF), F32),
            pltpu.VMEM((2, 8, HALF), F32),
            pltpu.VMEM((6, D, HALF), BF16),
            pltpu.VMEM((6, 8, HALF), F32),
            pltpu.VMEM((2, D, HALF), BF16),
            pltpu.VMEM((2, 8, HALF), F32),
            pltpu.VMEM((4, D, HALF), BF16),
            pltpu.VMEM((4, 8, HALF), F32),
        ] + [dma((6,))] * 8,
        compiler_params=pltpu.CompilerParams(
            collective_id=0, has_side_effects=True, vmem_limit_bytes=40 * 2**20),
        cost_estimate=pl.CostEstimate(flops=8 * 4096 * 4096 * 64, bytes_accessed=2**21, transcendentals=2**24),
    )(queries, prefix_keys, prefix_values, own_keys, own_values, lengths)


def solution(mesh):
    rows = P(("scene", "ctx"), "tp")
    return jax.shard_map(
        shards,
        mesh=mesh,
        in_specs=(rows, rows, rows, rows, rows, P(("scene", "ctx"))),
        out_specs=rows,
        check_vma=False,
    )
```

```python
import math

import jax
import jax.numpy as jnp
from jax import lax
from jax.experimental import pallas as pl
from jax.experimental.pallas import tpu as pltpu
from jax.sharding import PartitionSpec as P

MESH = pl.DeviceIdType.MESH
F32, BF16 = jnp.float32, jnp.bfloat16
D = 128
H = 8
T = 128
ROWS = 1024
HALF = 512
PART = 256
SIDE = 4
SCALE = math.log2(math.e) / math.sqrt(D)


ORDER = ((0, 0), (1, 0), (2, 0), (1, 1), (2, 1), (3, 0), (3, 1), (3, 2),
         (1, 2), (3, 3), (1, 3), (2, 2), (2, 3), (0, 1), (0, 2), (0, 3))
BLOCKS = len(ORDER)


def block_of(i):
    if isinstance(i, int):
        return ORDER[i]
    found = list(ORDER[0])
    for k in range(1, BLOCKS):
        reached = lax.div(i + (BLOCKS - k), BLOCKS)
        for part in range(2):
            step = ORDER[k][part] - ORDER[k - 1][part]
            if step:
                found[part] = found[part] + step * reached
    return found


def kernel(q_hbm, k_hbm, v_hbm, ok_hbm, ov_hbm, len_ref, out_ref,
           q, kb, vb, ok, ov, acc, mx, sm, s0, s1, x0, x1,
           o_send, st_send, o_recv, st_recv,
           in_sem, q_ssem, q_rsem, k_ssem, k_rsem, v_ssem, v_rsem, o_ssem, o_rsem, st_ssem, st_rsem):
    me = lax.axis_index("ctx")
    y, x = lax.div(me, SIDE), lax.rem(me, SIDE)
    turn = lax.axis_index("scene")

    def at(dx, dy):
        return lax.rem(y + dy, SIDE) * SIDE + lax.rem(x + dx, SIDE)

    right, left = at(1 - turn, turn), at((1 - turn) * 3, turn * 3)
    up, down = at(turn, 1 - turn), at(turn * 3, (1 - turn) * 3)
    far = at((1 - turn) * 2, turn * 2)

    def half(n):
        return pl.ds(n * HALF, HALF)

    loads = [
        pltpu.make_async_copy(q_hbm.at[:, half(0)], q.at[0], in_sem.at[0]),
        pltpu.make_async_copy(q_hbm.at[:, half(1)], q.at[1], in_sem.at[1]),
        pltpu.make_async_copy(k_hbm, kb.at[0], in_sem.at[2]),
        pltpu.make_async_copy(ok_hbm, ok, in_sem.at[3]),
        pltpu.make_async_copy(ov_hbm, ov, in_sem.at[4]),
        pltpu.make_async_copy(v_hbm, vb.at[0], in_sem.at[5]),
    ]
    for load in loads:
        load.start()
    barrier = pltpu.get_barrier_semaphore()
    for other in (left, right, up, down, far):
        pl.semaphore_signal(barrier, inc=1, device_id={"ctx": other}, device_id_type=MESH)

    def remote(src, dst, ssem, rsem, to):
        return pltpu.make_async_remote_copy(
            src_ref=src, dst_ref=dst, send_sem=ssem, recv_sem=rsem,
            device_id={"ctx": to}, device_id_type=MESH)

    def q_copy(n):
        dst, to = 2 + n, (right, left)[n % 2]
        src = q.at[n - 2] if n > 3 else q_hbm.at[:, half((0, 1, 1, 0)[n])]
        return remote(src, q.at[dst], q_ssem.at[n], q_rsem.at[n], to)

    def ring_copy(n, hbm, buf, ssem, rsem):
        place, to = half(n % 2), (up, down)[n % 2]
        src = buf.at[1, place] if n > 3 else hbm.at[half((0, 1, 1, 0)[n])]
        return remote(src, buf.at[1 + n // 2, place], ssem.at[n], rsem.at[n], to)

    def k_copy(n):
        return ring_copy(n, k_hbm, kb, k_ssem, k_rsem)

    def v_copy(n):
        return ring_copy(n, v_hbm, vb, v_ssem, v_rsem)

    def o_copy(n):
        to = (far, far, right, right, left, left)[n]
        return (remote(o_send.at[n], o_recv.at[n], o_ssem.at[n], o_rsem.at[n], to),
                remote(st_send.at[n], st_recv.at[n], st_ssem.at[n], st_rsem.at[n], to))

    def send_o(n, unit):
        o_send[n] = acc[unit].astype(BF16)
        for h in range(4):
            cols = slice(h * T, (h + 1) * T)
            st_send[n, h:h + 1, :] = mx[unit, 0:1, cols]
            st_send[n, 4 + h:5 + h, :] = sm[unit, 0:1, cols]
        for c in o_copy(n):
            c.start()

    def merge(unit, n):
        for c in o_copy(n):
            c.wait_recv()
        m, l = mx[unit, 0:1], sm[unit, 0:1]
        m2 = jnp.concatenate([st_recv[n, h:h + 1, :] for h in range(4)], axis=1)
        l2 = jnp.concatenate([st_recv[n, h:h + 1, :] for h in range(4, 8)], axis=1)
        new = jnp.maximum(m, m2)
        a, a2 = jnp.exp2((m - new) * SCALE), jnp.exp2((m2 - new) * SCALE)
        acc[unit] = acc[unit] * a + o_recv[n].astype(F32) * a2
        sm[unit, 0:1] = l * a + l2 * a2
        mx[unit, 0:1] = new

    def rows_of(unit, lo, hi):
        return jnp.concatenate([q[unit, :, h * D:(h + 1) * D] for h in range(lo, hi)], axis=0)

    def dot(a, b, da, db):
        return lax.dot_general(a, b, (((da,), (db,)), ((), ())), preferred_element_type=F32)

    def scores(i, u, s_ref, x_ref):
        slot, pair = block_of(i)
        cols = slice(u * PART, (u + 1) * PART)
        s = dot(kb[pair], rows_of(2 * slot + u // 2, 2 * (u % 2), 2 * (u % 2) + 2), 1, 1)
        s_ref[:, cols] = s
        x_ref[:, cols] = jnp.broadcast_to(jnp.max(s, axis=0, keepdims=True), (8, PART))

    def absorb(i, u, s_ref, x_ref):
        slot, pair = block_of(i)
        unit, cols = 2 * slot + u // 2, slice(u % 2 * PART, (u % 2 + 1) * PART)
        here = slice(u * PART, (u + 1) * PART)
        m, l = mx[unit, 0:1, cols], sm[unit, 0:1, cols]
        new = jnp.maximum(m, x_ref[0:1, here])
        p = jnp.exp2(s_ref[:, here] * SCALE - new * SCALE)
        a = jnp.exp2((m - new) * SCALE)
        d = dot(vb[pair], p.astype(BF16), 0, 0)
        sm[unit, 0:1, cols] = l * a + jnp.sum(p, axis=0, keepdims=True)
        acc[unit, :, cols] = acc[unit, :, cols] * a + d
        mx[unit, 0:1, cols] = new

    def block(i, cur, nxt):
        for u in range(4):
            if nxt is not None:
                scores(i + 1, u, *nxt)
            absorb(i, u, *cur)

    pl.semaphore_wait(barrier, 5)
    for n in range(4):
        q_copy(n).start()
    for n in range(2, 8):
        acc[n] = jnp.zeros((D, HALF), F32)
        mx[n, 0:1] = jnp.full((1, HALF), -1e30, F32)
        sm[n, 0:1] = jnp.zeros((1, HALF), F32)
    for n in range(5):
        loads[n].wait()

    length = len_ref[0]
    key_at = lax.broadcasted_iota(jnp.int32, (T, HALF), 0)
    token = lax.rem(lax.broadcasted_iota(jnp.int32, (T, HALF), 1), T)
    visible = (key_at <= token) & (key_at < length)
    for n in range(2):
        s = jnp.where(visible, dot(ok[...], rows_of(n, 0, 4), 1, 1), -1e30)
        m = jnp.max(s, axis=0, keepdims=True)
        p = jnp.exp2(s * SCALE - m * SCALE)
        acc[n] = dot(ov[...], p.astype(BF16), 0, 0)
        mx[n, 0:1] = m
        sm[n, 0:1] = jnp.sum(p, axis=0, keepdims=True)
    for u in range(4):
        scores(0, u, s0, x0)
    for n in range(4):
        k_copy(n).start()
        v_copy(n).start()
    loads[5].wait()

    even, odd = (s0, x0), (s1, x1)

    def receive(copy, *numbers):
        for n in numbers:
            copy(n).wait_recv()

    def q_needed(slot):
        if slot == 1:
            receive(q_copy, 0, 1)
            q_copy(4).start()
            q_copy(5).start()
        else:
            receive(q_copy, *((2, 3) if slot == 2 else (4, 5)))

    def ring_needed(copy, pair):
        receive(copy, 2 * pair - 2, 2 * pair - 1)
        if pair == 1:
            copy(4).start()
            copy(5).start()

    def send_slot(slot):
        for n, unit in (((2, 3), (4, 2)), ((3, 5), (5, 4)), ((0, 6), (1, 7)))[slot - 1]:
            send_o(n, unit)

    def before(i):
        todo = []
        if i > 0:
            done = ORDER[i - 1][0]
            if done > 0 and all(slot != done for slot, _ in ORDER[i:]):
                todo.append((send_slot, done))
        slot, pair = ORDER[i]
        if pair > 0 and all(p != pair for _, p in ORDER[:i]):
            todo.append((lambda p: ring_needed(v_copy, p), pair))
        if i + 1 < BLOCKS:
            slot, pair = ORDER[i + 1]
            if slot > 0 and all(t != slot for t, _ in ORDER[:i + 1]):
                todo.append((q_needed, slot))
            if pair > 0 and all(p != pair for _, p in ORDER[:i + 1]):
                todo.append((lambda p: ring_needed(k_copy, p), pair))
        return todo

    def body(j, carry):
        for parity, (cur, nxt) in enumerate(((even, odd), (odd, even))):
            for k in range(BLOCKS // 2 - 1):
                todo = before(2 * k + parity)
                if todo:
                    @pl.when(j == k)
                    def _():
                        for act, what in todo:
                            act(what)
            block(2 * j + parity, cur, nxt)
        return carry

    lax.fori_loop(0, BLOCKS // 2 - 1, body, 0)
    for i, cur, nxt in ((BLOCKS - 2, even, odd), (BLOCKS - 1, odd, None)):
        for act, what in before(i):
            act(what)
        block(i, cur, nxt)
    for unit, n in ((0, 0), (1, 1), (0, 4), (1, 2)):
        merge(unit, n)

    rows = lax.broadcasted_iota(jnp.int32, (T, D), 0)
    for unit, n in ((0, 3), (1, 5)):
        merge(unit, n)
        result = acc[unit] / sm[unit, 0:1]
        for h in range(4):
            piece = result[:, h * T:(h + 1) * T].T
            lo = (unit * 4 + h) * D
            out_ref[:, lo:lo + D] = jnp.where(rows < length, piece, 0.0).astype(BF16)

    for n in range(6):
        for c in (q_copy(n), k_copy(n), v_copy(n), *o_copy(n)):
            c.wait_send()


def shards(queries, prefix_keys, prefix_values, own_keys, own_values, lengths):
    dma = pltpu.SemaphoreType.DMA
    return pl.pallas_call(
        kernel,
        out_shape=jax.ShapeDtypeStruct((T, H * D), BF16),
        in_specs=[pl.BlockSpec(memory_space=pltpu.HBM)] * 5 + [pl.BlockSpec(memory_space=pltpu.SMEM)],
        out_specs=pl.BlockSpec(memory_space=pltpu.VMEM),
        scratch_shapes=[
            pltpu.VMEM((8, T, HALF), BF16),
            pltpu.VMEM((4, ROWS, D), BF16),
            pltpu.VMEM((4, ROWS, D), BF16),
            pltpu.VMEM((T, D), BF16),
            pltpu.VMEM((T, D), BF16),
            pltpu.VMEM((8, D, HALF), F32),
            pltpu.VMEM((8, 8, HALF), F32),
            pltpu.VMEM((8, 8, HALF), F32),
            pltpu.VMEM((ROWS, 2 * HALF), F32),
            pltpu.VMEM((ROWS, 2 * HALF), F32),
            pltpu.VMEM((8, 2 * HALF), F32),
            pltpu.VMEM((8, 2 * HALF), F32),
            pltpu.VMEM((6, D, HALF), BF16),
            pltpu.VMEM((6, 8, T), F32),
            pltpu.VMEM((6, D, HALF), BF16),
            pltpu.VMEM((6, 8, T), F32),
        ] + [dma((6,))] * 11,
        compiler_params=pltpu.CompilerParams(
            collective_id=0, has_side_effects=True, vmem_limit_bytes=62 * 2**20),
        cost_estimate=pl.CostEstimate(flops=2**33, bytes_accessed=2**21, transcendentals=2**24),
    )(queries, prefix_keys, prefix_values, own_keys, own_values, lengths)


def solution(mesh):
    rows = P(("scene", "ctx"), "tp")
    return jax.shard_map(
        shards,
        mesh=mesh,
        in_specs=(rows, rows, rows, rows, rows, P(("scene", "ctx"))),
        out_specs=rows,
        check_vma=False,
    )
```

```python
import math

import jax
import jax.numpy as jnp
from jax import lax
from jax.experimental import pallas as pl
from jax.experimental.pallas import tpu as pltpu
from jax.sharding import PartitionSpec as P

MESH = pl.DeviceIdType.MESH
F32, BF16 = jnp.float32, jnp.bfloat16
D = 128
H = 8
T = 128
ROWS = 1024
HALF = 512
PART = 256
SIDE = 4
SCALE = math.log2(math.e) / math.sqrt(D)


ORDER = ((0, 0), (1, 0), (2, 0), (1, 1), (2, 1), (3, 0), (3, 1), (3, 2),
         (1, 2), (3, 3), (1, 3), (2, 2), (2, 3), (0, 1), (0, 2), (0, 3))
BLOCKS = len(ORDER)


def block_of(i):
    if isinstance(i, int):
        return ORDER[i]
    found = list(ORDER[0])
    for k in range(1, BLOCKS):
        reached = lax.div(i + (BLOCKS - k), BLOCKS)
        for part in range(2):
            step = ORDER[k][part] - ORDER[k - 1][part]
            if step:
                found[part] = found[part] + step * reached
    return found


def kernel(q_hbm, k_hbm, v_hbm, okv_hbm, len_hbm, out_hbm,
           len_ref, out, q, kb, vb, ok, ov, acc, mx, sm, s0, s1, x0, x1,
           o_send, st_send, o_recv, st_recv,
           in_sem, q_ssem, q_rsem, k_ssem, k_rsem, v_ssem, v_rsem, o_ssem, o_rsem, st_ssem, st_rsem):
    me = lax.axis_index("ctx")
    y, x = lax.div(me, SIDE), lax.rem(me, SIDE)
    turn = lax.axis_index("scene")

    def at(dx, dy):
        return lax.rem(y + dy, SIDE) * SIDE + lax.rem(x + dx, SIDE)

    right, left = at(1 - turn, turn), at((1 - turn) * 3, turn * 3)
    up, down = at(turn, 1 - turn), at(turn * 3, (1 - turn) * 3)
    far = at((1 - turn) * 2, turn * 2)

    def half(n):
        return pl.ds(n * HALF, HALF)

    loads = [
        pltpu.make_async_copy(q_hbm.at[:, half(0)], q.at[0], in_sem.at[0]),
        pltpu.make_async_copy(q_hbm.at[:, half(1)], q.at[1], in_sem.at[1]),
        pltpu.make_async_copy(k_hbm, kb.at[0], in_sem.at[2]),
        pltpu.make_async_copy(okv_hbm.at[pl.ds(0, T)], ok, in_sem.at[3]),
        pltpu.make_async_copy(okv_hbm.at[pl.ds(T, T)], ov, in_sem.at[4]),
        pltpu.make_async_copy(len_hbm, len_ref, in_sem.at[5]),
        pltpu.make_async_copy(v_hbm, vb.at[0], in_sem.at[6]),
    ]
    for load in loads:
        load.start()
    barrier = pltpu.get_barrier_semaphore()
    for other in (left, right, up, down, far):
        pl.semaphore_signal(barrier, inc=1, device_id={"ctx": other}, device_id_type=MESH)

    def remote(src, dst, ssem, rsem, to):
        return pltpu.make_async_remote_copy(
            src_ref=src, dst_ref=dst, send_sem=ssem, recv_sem=rsem,
            device_id={"ctx": to}, device_id_type=MESH)

    def q_copy(n):
        dst, to = 2 + n, (right, left)[n % 2]
        src = q.at[n - 2] if n > 3 else q_hbm.at[:, half((0, 1, 1, 0)[n])]
        return remote(src, q.at[dst], q_ssem.at[n], q_rsem.at[n], to)

    def ring_copy(n, hbm, buf, ssem, rsem):
        place, to = half(n % 2), (up, down)[n % 2]
        src = buf.at[1, place] if n > 3 else hbm.at[half((0, 1, 1, 0)[n])]
        return remote(src, buf.at[1 + n // 2, place], ssem.at[n], rsem.at[n], to)

    def k_copy(n):
        return ring_copy(n, k_hbm, kb, k_ssem, k_rsem)

    def v_copy(n):
        return ring_copy(n, v_hbm, vb, v_ssem, v_rsem)

    def o_copy(n):
        to = (far, far, right, right, left, left)[n]
        return (remote(o_send.at[n], o_recv.at[n], o_ssem.at[n], o_rsem.at[n], to),
                remote(st_send.at[n], st_recv.at[n], st_ssem.at[n], st_rsem.at[n], to))

    def send_o(n, unit):
        o_send[n] = acc[unit].astype(BF16)
        for h in range(4):
            cols = slice(h * T, (h + 1) * T)
            st_send[n, h:h + 1, :] = mx[unit, 0:1, cols]
            st_send[n, 4 + h:5 + h, :] = sm[unit, 0:1, cols]
        for c in o_copy(n):
            c.start()

    def merge(unit, n):
        for c in o_copy(n):
            c.wait_recv()
        m, l = mx[unit, 0:1], sm[unit, 0:1]
        m2 = jnp.concatenate([st_recv[n, h:h + 1, :] for h in range(4)], axis=1)
        l2 = jnp.concatenate([st_recv[n, h:h + 1, :] for h in range(4, 8)], axis=1)
        new = jnp.maximum(m, m2)
        a, a2 = jnp.exp2((m - new) * SCALE), jnp.exp2((m2 - new) * SCALE)
        acc[unit] = acc[unit] * a + o_recv[n].astype(F32) * a2
        sm[unit, 0:1] = l * a + l2 * a2
        mx[unit, 0:1] = new

    def rows_of(unit, lo, hi):
        return jnp.concatenate([q[unit, :, h * D:(h + 1) * D] for h in range(lo, hi)], axis=0)

    def dot(a, b, da, db):
        return lax.dot_general(a, b, (((da,), (db,)), ((), ())), preferred_element_type=F32)

    def scores(i, u, s_ref, x_ref):
        slot, pair = block_of(i)
        cols = slice(u * PART, (u + 1) * PART)
        s = dot(kb[pair], rows_of(2 * slot + u // 2, 2 * (u % 2), 2 * (u % 2) + 2), 1, 1)
        s_ref[:, cols] = s
        x_ref[:, cols] = jnp.broadcast_to(jnp.max(s, axis=0, keepdims=True), (8, PART))

    def absorb(i, u, s_ref, x_ref):
        slot, pair = block_of(i)
        unit, cols = 2 * slot + u // 2, slice(u % 2 * PART, (u % 2 + 1) * PART)
        here = slice(u * PART, (u + 1) * PART)
        m, l = mx[unit, 0:1, cols], sm[unit, 0:1, cols]
        new = jnp.maximum(m, x_ref[0:1, here])
        p = jnp.exp2(s_ref[:, here] * SCALE - new * SCALE)
        a = jnp.exp2((m - new) * SCALE)
        d = dot(vb[pair], p.astype(BF16), 0, 0)
        sm[unit, 0:1, cols] = l * a + jnp.sum(p, axis=0, keepdims=True)
        acc[unit, :, cols] = acc[unit, :, cols] * a + d
        mx[unit, 0:1, cols] = new

    def block(i, cur, nxt):
        for u in range(4):
            if nxt is not None:
                scores(i + 1, u, *nxt)
            absorb(i, u, *cur)

    pl.semaphore_wait(barrier, 5)
    for n in range(4):
        q_copy(n).start()
    for n in range(2, 8):
        acc[n] = jnp.zeros((D, HALF), F32)
        mx[n, 0:1] = jnp.full((1, HALF), -1e30, F32)
        sm[n, 0:1] = jnp.zeros((1, HALF), F32)
    for n in range(6):
        loads[n].wait()

    length = len_ref[0]
    key_at = lax.broadcasted_iota(jnp.int32, (T, HALF), 0)
    token = lax.rem(lax.broadcasted_iota(jnp.int32, (T, HALF), 1), T)
    visible = (key_at <= token) & (key_at < length)
    for n in range(2):
        s = jnp.where(visible, dot(ok[...], rows_of(n, 0, 4), 1, 1), -1e30)
        m = jnp.max(s, axis=0, keepdims=True)
        p = jnp.exp2(s * SCALE - m * SCALE)
        acc[n] = dot(ov[...], p.astype(BF16), 0, 0)
        mx[n, 0:1] = m
        sm[n, 0:1] = jnp.sum(p, axis=0, keepdims=True)
    for u in range(4):
        scores(0, u, s0, x0)
    for n in range(4):
        k_copy(n).start()
        v_copy(n).start()
    loads[6].wait()

    even, odd = (s0, x0), (s1, x1)

    def receive(copy, *numbers):
        for n in numbers:
            copy(n).wait_recv()

    def q_needed(slot):
        if slot == 1:
            receive(q_copy, 0, 1)
            q_copy(4).start()
            q_copy(5).start()
        else:
            receive(q_copy, *((2, 3) if slot == 2 else (4, 5)))

    def ring_needed(copy, pair):
        receive(copy, 2 * pair - 2, 2 * pair - 1)
        if pair == 1:
            copy(4).start()
            copy(5).start()

    def send_slot(slot):
        for n, unit in (((2, 3), (4, 2)), ((3, 5), (5, 4)), ((0, 6), (1, 7)))[slot - 1]:
            send_o(n, unit)

    def before(i):
        todo = []
        if i > 0:
            done = ORDER[i - 1][0]
            if done > 0 and all(slot != done for slot, _ in ORDER[i:]):
                todo.append((send_slot, done))
        slot, pair = ORDER[i]
        if pair > 0 and all(p != pair for _, p in ORDER[:i]):
            todo.append((lambda p: ring_needed(v_copy, p), pair))
        if i + 1 < BLOCKS:
            slot, pair = ORDER[i + 1]
            if slot > 0 and all(t != slot for t, _ in ORDER[:i + 1]):
                todo.append((q_needed, slot))
            if pair > 0 and all(p != pair for _, p in ORDER[:i + 1]):
                todo.append((lambda p: ring_needed(k_copy, p), pair))
        return todo

    def body(j, carry):
        for parity, (cur, nxt) in enumerate(((even, odd), (odd, even))):
            for k in range(BLOCKS // 2 - 1):
                todo = before(2 * k + parity)
                if todo:
                    @pl.when(j == k)
                    def _():
                        for act, what in todo:
                            act(what)
            block(2 * j + parity, cur, nxt)
        return carry

    lax.fori_loop(0, BLOCKS // 2 - 1, body, 0)
    for i, cur, nxt in ((BLOCKS - 2, even, odd), (BLOCKS - 1, odd, None)):
        for act, what in before(i):
            act(what)
        block(i, cur, nxt)
    for unit, n in ((0, 0), (1, 1), (0, 4), (1, 2)):
        merge(unit, n)

    rows = lax.broadcasted_iota(jnp.int32, (T, D), 0)
    writes = []
    for unit, n in ((0, 3), (1, 5)):
        merge(unit, n)
        result = acc[unit] / sm[unit, 0:1]
        for h in range(4):
            piece = result[:, h * T:(h + 1) * T].T
            out[:, (unit * 4 + h) * D:(unit * 4 + h + 1) * D] = jnp.where(rows < length, piece, 0.0).astype(BF16)
        write = pltpu.make_async_copy(out.at[:, half(unit)], out_hbm.at[:, half(unit)], in_sem.at[7 + unit])
        write.start()
        writes.append(write)
    for write in writes:
        write.wait()

    for n in range(6):
        for c in (q_copy(n), k_copy(n), v_copy(n), *o_copy(n)):
            c.wait_send()


def shards(queries, prefix_keys, prefix_values, own_keys, own_values, lengths):
    dma = pltpu.SemaphoreType.DMA
    return pl.pallas_call(
        kernel,
        out_shape=jax.ShapeDtypeStruct((T, H * D), BF16),
        in_specs=[pl.BlockSpec(memory_space=pltpu.HBM)] * 5,
        out_specs=pl.BlockSpec(memory_space=pltpu.HBM),
        scratch_shapes=[
            pltpu.SMEM((1,), jnp.int32),
            pltpu.VMEM((T, H * D), BF16),
            pltpu.VMEM((8, T, HALF), BF16),
            pltpu.VMEM((4, ROWS, D), BF16),
            pltpu.VMEM((4, ROWS, D), BF16),
            pltpu.VMEM((T, D), BF16),
            pltpu.VMEM((T, D), BF16),
            pltpu.VMEM((8, D, HALF), F32),
            pltpu.VMEM((8, 8, HALF), F32),
            pltpu.VMEM((8, 8, HALF), F32),
            pltpu.VMEM((ROWS, 2 * HALF), F32),
            pltpu.VMEM((ROWS, 2 * HALF), F32),
            pltpu.VMEM((8, 2 * HALF), F32),
            pltpu.VMEM((8, 2 * HALF), F32),
            pltpu.VMEM((6, D, HALF), BF16),
            pltpu.VMEM((6, 8, T), F32),
            pltpu.VMEM((6, D, HALF), BF16),
            pltpu.VMEM((6, 8, T), F32),
        ] + [dma((9,))] + [dma((6,))] * 10,
        compiler_params=pltpu.CompilerParams(
            collective_id=0, has_side_effects=True, vmem_limit_bytes=5355 * 2**20 // 100),
        cost_estimate=pl.CostEstimate(flops=2**33, bytes_accessed=2**21, transcendentals=2**24),
    )(queries, prefix_keys, prefix_values, jnp.concatenate([own_keys, own_values], axis=0), lengths)


def solution(mesh):
    rows = P(("scene", "ctx"), "tp")
    return jax.shard_map(
        shards,
        mesh=mesh,
        in_specs=(rows, rows, rows, rows, rows, P(("scene", "ctx"))),
        out_specs=rows,
        check_vma=False,
    )
```

```python
import math

import jax
import jax.numpy as jnp
from jax import lax
from jax.experimental import pallas as pl
from jax.experimental.pallas import tpu as pltpu
from jax.sharding import PartitionSpec as P

MESH = pl.DeviceIdType.MESH
F32, BF16 = jnp.float32, jnp.bfloat16
D = 128
H = 8
T = 128
ROWS = 1024
HALF = 512
PART = 256
SIDE = 4
SCALE = math.log2(math.e) / math.sqrt(D)


ORDER = ((0, 0), (1, 0), (2, 0), (1, 1), (2, 1), (3, 0), (3, 1), (3, 2), (3, 3), (1, 2), (1, 3), (2, 2), (2, 3), (0, 1), (0, 2), (0, 3))
BLOCKS = len(ORDER)


def block_of(i):
    if isinstance(i, int):
        return ORDER[i]
    found = list(ORDER[0])
    for k in range(1, BLOCKS):
        reached = lax.div(i + (BLOCKS - k), BLOCKS)
        for part in range(2):
            step = ORDER[k][part] - ORDER[k - 1][part]
            if step:
                found[part] = found[part] + step * reached
    return found


def kernel(q_hbm, k_hbm, v_hbm, okv_hbm, len_hbm, out_hbm,
           len_ref, out, q, kb, vb, ok, ov, acc, mx, sm, s0, s1, x0, x1,
           o_send, st_send, o_recv, st_recv,
           in_sem, q_ssem, q_rsem, k_ssem, k_rsem, v_ssem, v_rsem, o_ssem, o_rsem, st_ssem, st_rsem):
    me = lax.axis_index("ctx")
    y, x = lax.div(me, SIDE), lax.rem(me, SIDE)
    turn = lax.axis_index("scene")

    def at(dx, dy):
        return lax.rem(y + dy, SIDE) * SIDE + lax.rem(x + dx, SIDE)

    right, left = at(1 - turn, turn), at((1 - turn) * 3, turn * 3)
    up, down = at(turn, 1 - turn), at(turn * 3, (1 - turn) * 3)
    far = at((1 - turn) * 2, turn * 2)

    def half(n):
        return pl.ds(n * HALF, HALF)

    loads = [
        pltpu.make_async_copy(q_hbm.at[:, half(0)], q.at[0], in_sem.at[0]),
        pltpu.make_async_copy(q_hbm.at[:, half(1)], q.at[1], in_sem.at[1]),
        pltpu.make_async_copy(k_hbm, kb.at[0], in_sem.at[2]),
        pltpu.make_async_copy(okv_hbm.at[pl.ds(0, T)], ok, in_sem.at[3]),
        pltpu.make_async_copy(okv_hbm.at[pl.ds(T, T)], ov, in_sem.at[4]),
        pltpu.make_async_copy(len_hbm, len_ref, in_sem.at[5]),
        pltpu.make_async_copy(v_hbm, vb.at[0], in_sem.at[6]),
    ]
    for load in loads:
        load.start()
    barrier = pltpu.get_barrier_semaphore()
    for other in (left, right, up, down, far):
        pl.semaphore_signal(barrier, inc=1, device_id={"ctx": other}, device_id_type=MESH)

    def remote(src, dst, ssem, rsem, to):
        return pltpu.make_async_remote_copy(
            src_ref=src, dst_ref=dst, send_sem=ssem, recv_sem=rsem,
            device_id={"ctx": to}, device_id_type=MESH)

    def q_copy(n):
        dst, to = 2 + n, (right, left)[n % 2]
        src = q.at[n - 2] if n > 3 else q_hbm.at[:, half((0, 1, 1, 0)[n])]
        return remote(src, q.at[dst], q_ssem.at[n], q_rsem.at[n], to)

    def ring_copy(n, hbm, buf, ssem, rsem):
        place, to = half(n % 2), (up, down)[n % 2]
        src = buf.at[1, place] if n > 3 else hbm.at[half((0, 1, 1, 0)[n])]
        return remote(src, buf.at[1 + n // 2, place], ssem.at[n], rsem.at[n], to)

    def k_copy(n):
        return ring_copy(n, k_hbm, kb, k_ssem, k_rsem)

    def v_copy(n):
        return ring_copy(n, v_hbm, vb, v_ssem, v_rsem)

    def o_copy(n):
        to = (far, far, right, right, left, left)[n]
        return (remote(o_send.at[n], o_recv.at[n], o_ssem.at[n], o_rsem.at[n], to),
                remote(st_send.at[n], st_recv.at[n], st_ssem.at[n], st_rsem.at[n], to))

    def send_o(n, unit):
        o_send[n] = acc[unit].astype(BF16)
        for h in range(4):
            cols = slice(h * T, (h + 1) * T)
            st_send[n, h:h + 1, :] = mx[unit, 0:1, cols]
            st_send[n, 4 + h:5 + h, :] = sm[unit, 0:1, cols]
        for c in o_copy(n):
            c.start()

    def merge(unit, n):
        for c in o_copy(n):
            c.wait_recv()
        m, l = mx[unit, 0:1], sm[unit, 0:1]
        m2 = jnp.concatenate([st_recv[n, h:h + 1, :] for h in range(4)], axis=1)
        l2 = jnp.concatenate([st_recv[n, h:h + 1, :] for h in range(4, 8)], axis=1)
        new = jnp.maximum(m, m2)
        a, a2 = jnp.exp2((m - new) * SCALE), jnp.exp2((m2 - new) * SCALE)
        acc[unit] = acc[unit] * a + o_recv[n].astype(F32) * a2
        sm[unit, 0:1] = l * a + l2 * a2
        mx[unit, 0:1] = new

    def rows_of(unit, lo, hi):
        return jnp.concatenate([q[unit, :, h * D:(h + 1) * D] for h in range(lo, hi)], axis=0)

    def dot(a, b, da, db):
        return lax.dot_general(a, b, (((da,), (db,)), ((), ())), preferred_element_type=F32)

    def scores(i, u, s_ref, x_ref):
        slot, pair = block_of(i)
        cols = slice(u * PART, (u + 1) * PART)
        s = dot(kb[pair], rows_of(2 * slot + u // 2, 2 * (u % 2), 2 * (u % 2) + 2), 1, 1)
        s_ref[:, cols] = s
        x_ref[:, cols] = jnp.broadcast_to(jnp.max(s, axis=0, keepdims=True), (8, PART))

    def absorb(i, u, s_ref, x_ref):
        slot, pair = block_of(i)
        unit, cols = 2 * slot + u // 2, slice(u % 2 * PART, (u % 2 + 1) * PART)
        here = slice(u * PART, (u + 1) * PART)
        m, l = mx[unit, 0:1, cols], sm[unit, 0:1, cols]
        new = jnp.maximum(m, x_ref[0:1, here])
        p = jnp.exp2(s_ref[:, here] * SCALE - new * SCALE)
        a = jnp.exp2((m - new) * SCALE)
        d = dot(vb[pair], p.astype(BF16), 0, 0)
        sm[unit, 0:1, cols] = l * a + jnp.sum(p, axis=0, keepdims=True)
        acc[unit, :, cols] = acc[unit, :, cols] * a + d
        mx[unit, 0:1, cols] = new

    def block(i, cur, nxt):
        for u in range(4):
            if nxt is not None:
                scores(i + 1, u, *nxt)
            absorb(i, u, *cur)

    pl.semaphore_wait(barrier, 5)
    for n in range(4):
        q_copy(n).start()
    for n in range(2, 8):
        acc[n] = jnp.zeros((D, HALF), F32)
        mx[n, 0:1] = jnp.full((1, HALF), -1e30, F32)
        sm[n, 0:1] = jnp.zeros((1, HALF), F32)
    for n in range(6):
        loads[n].wait()

    length = len_ref[0]
    key_at = lax.broadcasted_iota(jnp.int32, (T, HALF), 0)
    token = lax.rem(lax.broadcasted_iota(jnp.int32, (T, HALF), 1), T)
    visible = (key_at <= token) & (key_at < length)
    for n in range(2):
        s = jnp.where(visible, dot(ok[...], rows_of(n, 0, 4), 1, 1), -1e30)
        m = jnp.max(s, axis=0, keepdims=True)
        p = jnp.exp2(s * SCALE - m * SCALE)
        acc[n] = dot(ov[...], p.astype(BF16), 0, 0)
        mx[n, 0:1] = m
        sm[n, 0:1] = jnp.sum(p, axis=0, keepdims=True)
    for u in range(4):
        scores(0, u, s0, x0)
    for n in range(4):
        k_copy(n).start()
        v_copy(n).start()
    loads[6].wait()

    even, odd = (s0, x0), (s1, x1)

    def receive(copy, *numbers):
        for n in numbers:
            copy(n).wait_recv()

    def q_needed(slot):
        if slot == 1:
            receive(q_copy, 0, 1)
            q_copy(4).start()
            q_copy(5).start()
        else:
            receive(q_copy, *((2, 3) if slot == 2 else (4, 5)))

    def ring_needed(copy, pair):
        receive(copy, 2 * pair - 2, 2 * pair - 1)
        if pair == 1:
            copy(4).start()
            copy(5).start()

    def send_slot(slot):
        for n, unit in (((2, 3), (4, 2)), ((3, 5), (5, 4)), ((0, 6), (1, 7)))[slot - 1]:
            send_o(n, unit)

    def before(i):
        todo = []
        if i > 0:
            done = ORDER[i - 1][0]
            if done > 0 and all(slot != done for slot, _ in ORDER[i:]):
                todo.append((send_slot, done))
        slot, pair = ORDER[i]
        if pair > 0 and all(p != pair for _, p in ORDER[:i]):
            todo.append((lambda p: ring_needed(v_copy, p), pair))
        if i + 1 < BLOCKS:
            slot, pair = ORDER[i + 1]
            if slot > 0 and all(t != slot for t, _ in ORDER[:i + 1]):
                todo.append((q_needed, slot))
            if pair > 0 and all(p != pair for _, p in ORDER[:i + 1]):
                todo.append((lambda p: ring_needed(k_copy, p), pair))
        return todo

    def body(j, carry):
        for parity, (cur, nxt) in enumerate(((even, odd), (odd, even))):
            for k in range(BLOCKS // 2 - 1):
                todo = before(2 * k + parity)
                if todo:
                    @pl.when(j == k)
                    def _():
                        for act, what in todo:
                            act(what)
            block(2 * j + parity, cur, nxt)
        return carry

    lax.fori_loop(0, BLOCKS // 2 - 1, body, 0)
    for i, cur, nxt in ((BLOCKS - 2, even, odd), (BLOCKS - 1, odd, None)):
        for act, what in before(i):
            act(what)
        block(i, cur, nxt)
    for unit, n in ((0, 0), (1, 1), (0, 4), (1, 2)):
        merge(unit, n)

    rows = lax.broadcasted_iota(jnp.int32, (T, D), 0)
    writes = []
    for unit, n in ((0, 3), (1, 5)):
        merge(unit, n)
        result = acc[unit] / sm[unit, 0:1]
        for h in range(4):
            piece = result[:, h * T:(h + 1) * T].T
            out[:, (unit * 4 + h) * D:(unit * 4 + h + 1) * D] = jnp.where(rows < length, piece, 0.0).astype(BF16)
        write = pltpu.make_async_copy(out.at[:, half(unit)], out_hbm.at[:, half(unit)], in_sem.at[7 + unit])
        write.start()
        writes.append(write)
    for write in writes:
        write.wait()

    for n in range(6):
        for c in (q_copy(n), k_copy(n), v_copy(n), *o_copy(n)):
            c.wait_send()


def shards(queries, prefix_keys, prefix_values, own_keys, own_values, lengths):
    dma = pltpu.SemaphoreType.DMA
    return pl.pallas_call(
        kernel,
        out_shape=jax.ShapeDtypeStruct((T, H * D), BF16),
        in_specs=[pl.BlockSpec(memory_space=pltpu.HBM)] * 5,
        out_specs=pl.BlockSpec(memory_space=pltpu.HBM),
        scratch_shapes=[
            pltpu.SMEM((1,), jnp.int32),
            pltpu.VMEM((T, H * D), BF16),
            pltpu.VMEM((8, T, HALF), BF16),
            pltpu.VMEM((4, ROWS, D), BF16),
            pltpu.VMEM((4, ROWS, D), BF16),
            pltpu.VMEM((T, D), BF16),
            pltpu.VMEM((T, D), BF16),
            pltpu.VMEM((8, D, HALF), F32),
            pltpu.VMEM((8, 8, HALF), F32),
            pltpu.VMEM((8, 8, HALF), F32),
            pltpu.VMEM((ROWS, 2 * HALF), F32),
            pltpu.VMEM((ROWS, 2 * HALF), F32),
            pltpu.VMEM((8, 2 * HALF), F32),
            pltpu.VMEM((8, 2 * HALF), F32),
            pltpu.VMEM((6, D, HALF), BF16),
            pltpu.VMEM((6, 8, T), F32),
            pltpu.VMEM((6, D, HALF), BF16),
            pltpu.VMEM((6, 8, T), F32),
        ] + [dma((9,))] + [dma((6,))] * 10,
        compiler_params=pltpu.CompilerParams(
            collective_id=0, has_side_effects=True, vmem_limit_bytes=5355 * 2**20 // 100),
        cost_estimate=pl.CostEstimate(flops=2**33, bytes_accessed=2**21, transcendentals=2**24),
    )(queries, prefix_keys, prefix_values, jnp.concatenate([own_keys, own_values], axis=0), lengths)


def solution(mesh):
    rows = P(("scene", "ctx"), "tp")
    return jax.shard_map(
        shards,
        mesh=mesh,
        in_specs=(rows, rows, rows, rows, rows, P(("scene", "ctx"))),
        out_specs=rows,
        check_vma=False,
    )
```

```python
import math

import jax
import jax.numpy as jnp
from jax import lax
from jax.experimental import pallas as pl
from jax.experimental.pallas import tpu as pltpu
from jax.sharding import PartitionSpec as P

MESH = pl.DeviceIdType.MESH
F32, BF16 = jnp.float32, jnp.bfloat16
D = 128
H = 8
T = 128
ROWS = 1024
HALF = 512
PART = 256
SIDE = 4
SCALE = math.log2(math.e) / math.sqrt(D)


ORDER = ((0, 0), (1, 0), (2, 0), (1, 1), (2, 1), (3, 0), (3, 1), (3, 2), (3, 3), (1, 2), (1, 3), (2, 2), (2, 3), (0, 1), (0, 2), (0, 3))
BLOCKS = len(ORDER)


def block_of(i):
    if isinstance(i, int):
        return ORDER[i]
    found = list(ORDER[0])
    for k in range(1, BLOCKS):
        reached = lax.div(i + (BLOCKS - k), BLOCKS)
        for part in range(2):
            step = ORDER[k][part] - ORDER[k - 1][part]
            if step:
                found[part] = found[part] + step * reached
    return found


def kernel(q_hbm, k_hbm, v_hbm, okv_hbm, len_hbm, out_hbm,
           len_ref, out, q, kb, vb, ok, ov, acc, mx, sm, s0, s1, x0, x1,
           o_send, st_send, o_recv, st_recv,
           in_sem, q_ssem, q_rsem, k_ssem, k_rsem, v_ssem, v_rsem, o_ssem, o_rsem, st_ssem, st_rsem):
    me = lax.axis_index("ctx")
    y, x = lax.div(me, SIDE), lax.rem(me, SIDE)
    turn = lax.axis_index("scene")

    def at(dx, dy):
        return lax.rem(y + dy, SIDE) * SIDE + lax.rem(x + dx, SIDE)

    right, left = at(1 - turn, turn), at((1 - turn) * 3, turn * 3)
    up, down = at(turn, 1 - turn), at(turn * 3, (1 - turn) * 3)
    far = at((1 - turn) * 2, turn * 2)

    def half(n):
        return pl.ds(n * HALF, HALF)

    loads = [
        pltpu.make_async_copy(q_hbm.at[:, half(0)], q.at[0], in_sem.at[0]),
        pltpu.make_async_copy(q_hbm.at[:, half(1)], q.at[1], in_sem.at[1]),
        pltpu.make_async_copy(k_hbm, kb.at[0], in_sem.at[2]),
        pltpu.make_async_copy(okv_hbm.at[pl.ds(0, T)], ok, in_sem.at[3]),
        pltpu.make_async_copy(okv_hbm.at[pl.ds(T, T)], ov, in_sem.at[4]),
        pltpu.make_async_copy(len_hbm, len_ref, in_sem.at[5]),
        pltpu.make_async_copy(v_hbm, vb.at[0], in_sem.at[6]),
    ]
    for load in loads:
        load.start()
    barrier = pltpu.get_barrier_semaphore()
    for other in (left, right, up, down, far):
        pl.semaphore_signal(barrier, inc=1, device_id={"ctx": other}, device_id_type=MESH)

    def remote(src, dst, ssem, rsem, to):
        return pltpu.make_async_remote_copy(
            src_ref=src, dst_ref=dst, send_sem=ssem, recv_sem=rsem,
            device_id={"ctx": to}, device_id_type=MESH)

    def q_copy(n):
        dst, to = 2 + n, (right, left)[n % 2]
        src = q.at[n - 2] if n > 3 else q_hbm.at[:, half((0, 1, 1, 0)[n])]
        return remote(src, q.at[dst], q_ssem.at[n], q_rsem.at[n], to)

    def ring_copy(n, hbm, buf, ssem, rsem):
        place, to = half(n % 2), (up, down)[n % 2]
        src = buf.at[1, place] if n > 3 else hbm.at[half((0, 1, 1, 0)[n])]
        return remote(src, buf.at[1 + n // 2, place], ssem.at[n], rsem.at[n], to)

    def k_copy(n):
        return ring_copy(n, k_hbm, kb, k_ssem, k_rsem)

    def v_copy(n):
        return ring_copy(n, v_hbm, vb, v_ssem, v_rsem)

    def o_copy(n):
        to = (far, far, right, right, left, left)[n]
        return (remote(o_send.at[n], o_recv.at[n], o_ssem.at[n], o_rsem.at[n], to),
                remote(st_send.at[n], st_recv.at[n], st_ssem.at[n], st_rsem.at[n], to))

    def send_o(n, unit):
        o_send[n] = acc[unit].astype(BF16)
        for h in range(4):
            cols = slice(h * T, (h + 1) * T)
            st_send[n, h:h + 1, :] = mx[unit, 0:1, cols]
            st_send[n, 4 + h:5 + h, :] = sm[unit, 0:1, cols]
        for c in o_copy(n):
            c.start()

    def merge(unit, n):
        for c in o_copy(n):
            c.wait_recv()
        m, l = mx[unit, 0:1], sm[unit, 0:1]
        m2 = jnp.concatenate([st_recv[n, h:h + 1, :] for h in range(4)], axis=1)
        l2 = jnp.concatenate([st_recv[n, h:h + 1, :] for h in range(4, 8)], axis=1)
        new = jnp.maximum(m, m2)
        a, a2 = jnp.exp2((m - new) * SCALE), jnp.exp2((m2 - new) * SCALE)
        acc[unit] = acc[unit] * a + o_recv[n].astype(F32) * a2
        sm[unit, 0:1] = l * a + l2 * a2
        mx[unit, 0:1] = new

    def rows_of(unit, lo, hi):
        return jnp.concatenate([q[unit, :, h * D:(h + 1) * D] for h in range(lo, hi)], axis=0)

    def dot(a, b, da, db):
        return lax.dot_general(a, b, (((da,), (db,)), ((), ())), preferred_element_type=F32)

    def scores(i, u, s_ref, x_ref):
        slot, pair = block_of(i)
        cols = slice(u * PART, (u + 1) * PART)
        s = dot(kb[pair], rows_of(2 * slot + u // 2, 2 * (u % 2), 2 * (u % 2) + 2), 1, 1)
        s_ref[:, cols] = s
        x_ref[:, cols] = jnp.broadcast_to(jnp.max(s, axis=0, keepdims=True), (8, PART))

    def absorb(i, u, s_ref, x_ref):
        slot, pair = block_of(i)
        unit, cols = 2 * slot + u // 2, slice(u % 2 * PART, (u % 2 + 1) * PART)
        here = slice(u * PART, (u + 1) * PART)
        m, l = mx[unit, 0:1, cols], sm[unit, 0:1, cols]
        new = jnp.maximum(m, x_ref[0:1, here])
        p = jnp.exp2(s_ref[:, here] * SCALE - new * SCALE)
        a = jnp.exp2((m - new) * SCALE)
        d = dot(vb[pair], p.astype(BF16), 0, 0)
        sm[unit, 0:1, cols] = l * a + jnp.sum(p, axis=0, keepdims=True)
        acc[unit, :, cols] = acc[unit, :, cols] * a + d
        mx[unit, 0:1, cols] = new

    def block(i, cur, nxt):
        for u in range(4):
            if nxt is not None:
                scores(i + 1, u, *nxt)
            absorb(i, u, *cur)

    pl.semaphore_wait(barrier, 5)
    for n in range(4):
        q_copy(n).start()
    for n in range(2, 8):
        acc[n] = jnp.zeros((D, HALF), F32)
        mx[n, 0:1] = jnp.full((1, HALF), -1e30, F32)
        sm[n, 0:1] = jnp.zeros((1, HALF), F32)
    for n in range(6):
        loads[n].wait()

    length = len_ref[0]
    key_at = lax.broadcasted_iota(jnp.int32, (T, HALF), 0)
    token = lax.rem(lax.broadcasted_iota(jnp.int32, (T, HALF), 1), T)
    visible = (key_at <= token) & (key_at < length)
    for n in range(2):
        s = jnp.where(visible, dot(ok[...], rows_of(n, 0, 4), 1, 1), -1e30)
        m = jnp.max(s, axis=0, keepdims=True)
        p = jnp.exp2(s * SCALE - m * SCALE)
        acc[n] = dot(ov[...], p.astype(BF16), 0, 0)
        mx[n, 0:1] = m
        sm[n, 0:1] = jnp.sum(p, axis=0, keepdims=True)
    for u in range(4):
        scores(0, u, s0, x0)
    loads[6].wait()

    even, odd = (s0, x0), (s1, x1)

    def receive(copy, *numbers):
        for n in numbers:
            copy(n).wait_recv()

    def q_needed(slot):
        if slot == 1:
            receive(q_copy, 0, 1)
            q_copy(4).start()
            q_copy(5).start()
        else:
            receive(q_copy, *((2, 3) if slot == 2 else (4, 5)))

    def ring_needed(copy, pair):
        receive(copy, 2 * pair - 2, 2 * pair - 1)
        if pair == 1:
            copy(4).start()
            copy(5).start()

    def send_slot(slot):
        for n, unit in (((2, 3), (4, 2)), ((3, 5), (5, 4)), ((0, 6), (1, 7)))[slot - 1]:
            send_o(n, unit)

    def before(i):
        todo = []
        if i > 0:
            done = ORDER[i - 1][0]
            if done > 0 and all(slot != done for slot, _ in ORDER[i:]):
                todo.append((send_slot, done))
        slot, pair = ORDER[i]
        if pair > 0 and all(p != pair for _, p in ORDER[:i]):
            todo.append((lambda p: ring_needed(v_copy, p), pair))
        if i + 1 < BLOCKS:
            slot, pair = ORDER[i + 1]
            if slot > 0 and all(t != slot for t, _ in ORDER[:i + 1]):
                todo.append((q_needed, slot))
            if pair > 0 and all(p != pair for _, p in ORDER[:i + 1]):
                todo.append((lambda p: ring_needed(k_copy, p), pair))
        return todo

    def body(j, carry):
        for parity, (cur, nxt) in enumerate(((odd, even), (even, odd))):
            for k in range(BLOCKS // 2 - 1):
                todo = before(1 + 2 * k + parity)
                if todo:
                    @pl.when(j == k)
                    def _():
                        for act, what in todo:
                            act(what)
            block(1 + 2 * j + parity, cur, nxt)
        return carry

    block(0, even, None)
    for n in range(4):
        k_copy(n).start()
        v_copy(n).start()
    for act, what in before(0):
        act(what)
    for u in range(4):
        scores(1, u, *odd)
    lax.fori_loop(0, BLOCKS // 2 - 1, body, 0)
    for act, what in before(BLOCKS - 1):
        act(what)
    block(BLOCKS - 1, odd, None)
    for unit, n in ((0, 0), (1, 1), (0, 4), (1, 2)):
        merge(unit, n)

    rows = lax.broadcasted_iota(jnp.int32, (T, D), 0)
    writes = []
    for unit, n in ((0, 3), (1, 5)):
        merge(unit, n)
        result = acc[unit] / sm[unit, 0:1]
        for h in range(4):
            piece = result[:, h * T:(h + 1) * T].T
            out[:, (unit * 4 + h) * D:(unit * 4 + h + 1) * D] = jnp.where(rows < length, piece, 0.0).astype(BF16)
        write = pltpu.make_async_copy(out.at[:, half(unit)], out_hbm.at[:, half(unit)], in_sem.at[7 + unit])
        write.start()
        writes.append(write)
    for write in writes:
        write.wait()

    for n in range(6):
        for c in (q_copy(n), k_copy(n), v_copy(n), *o_copy(n)):
            c.wait_send()


def shards(queries, prefix_keys, prefix_values, own_keys, own_values, lengths):
    dma = pltpu.SemaphoreType.DMA
    return pl.pallas_call(
        kernel,
        out_shape=jax.ShapeDtypeStruct((T, H * D), BF16),
        in_specs=[pl.BlockSpec(memory_space=pltpu.HBM)] * 5,
        out_specs=pl.BlockSpec(memory_space=pltpu.HBM),
        scratch_shapes=[
            pltpu.SMEM((1,), jnp.int32),
            pltpu.VMEM((T, H * D), BF16),
            pltpu.VMEM((8, T, HALF), BF16),
            pltpu.VMEM((4, ROWS, D), BF16),
            pltpu.VMEM((4, ROWS, D), BF16),
            pltpu.VMEM((T, D), BF16),
            pltpu.VMEM((T, D), BF16),
            pltpu.VMEM((8, D, HALF), F32),
            pltpu.VMEM((8, 8, HALF), F32),
            pltpu.VMEM((8, 8, HALF), F32),
            pltpu.VMEM((ROWS, 2 * HALF), F32),
            pltpu.VMEM((ROWS, 2 * HALF), F32),
            pltpu.VMEM((8, 2 * HALF), F32),
            pltpu.VMEM((8, 2 * HALF), F32),
            pltpu.VMEM((6, D, HALF), BF16),
            pltpu.VMEM((6, 8, T), F32),
            pltpu.VMEM((6, D, HALF), BF16),
            pltpu.VMEM((6, 8, T), F32),
        ] + [dma((9,))] + [dma((6,))] * 10,
        compiler_params=pltpu.CompilerParams(
            collective_id=0, has_side_effects=True, vmem_limit_bytes=5355 * 2**20 // 100),
        cost_estimate=pl.CostEstimate(flops=2**33, bytes_accessed=2**21, transcendentals=2**24),
    )(queries, prefix_keys, prefix_values, jnp.concatenate([own_keys, own_values], axis=0), lengths)


def solution(mesh):
    rows = P(("scene", "ctx"), "tp")
    return jax.shard_map(
        shards,
        mesh=mesh,
        in_specs=(rows, rows, rows, rows, rows, P(("scene", "ctx"))),
        out_specs=rows,
        check_vma=False,
    )
```

```python
import math

import jax
import jax.numpy as jnp
from jax import lax
from jax.experimental import pallas as pl
from jax.experimental.pallas import tpu as pltpu
from jax.sharding import PartitionSpec as P

MESH = pl.DeviceIdType.MESH
F32, BF16 = jnp.float32, jnp.bfloat16
D = 128
H = 8
T = 128
ROWS = 1024
HALF = 512
PART = 256
SIDE = 4
SCALE = math.log2(math.e) / math.sqrt(D)


ORDER = ((0, 0), (1, 0), (2, 0), (1, 1), (2, 1), (3, 0), (3, 1), (3, 2), (3, 3), (1, 2), (1, 3), (2, 2), (2, 3), (0, 1), (0, 2), (0, 3))
BLOCKS = len(ORDER)


def block_of(i):
    if isinstance(i, int):
        return ORDER[i]
    found = list(ORDER[0])
    for k in range(1, BLOCKS):
        reached = lax.div(i + (BLOCKS - k), BLOCKS)
        for part in range(2):
            step = ORDER[k][part] - ORDER[k - 1][part]
            if step:
                found[part] = found[part] + step * reached
    return found


def kernel(q_hbm, k_hbm, v_hbm, okv_hbm, len_hbm, out_hbm,
           len_ref, out, q, kb, vb, ok, ov, acc, mx, sm, s0, s1, x0, x1,
           o_send, st_send, o_recv, st_recv,
           in_sem, q_ssem, q_rsem, k_ssem, k_rsem, v_ssem, v_rsem, o_ssem, o_rsem, st_ssem, st_rsem):
    me = lax.axis_index("ctx")
    y, x = lax.div(me, SIDE), lax.rem(me, SIDE)
    turn = lax.axis_index("scene")

    def at(dx, dy):
        return lax.rem(y + dy, SIDE) * SIDE + lax.rem(x + dx, SIDE)

    right, left = at(1 - turn, turn), at((1 - turn) * 3, turn * 3)
    up, down = at(turn, 1 - turn), at(turn * 3, (1 - turn) * 3)
    far = at((1 - turn) * 2, turn * 2)

    def half(n):
        return pl.ds(n * HALF, HALF)

    loads = [
        pltpu.make_async_copy(q_hbm.at[:, half(0)], q.at[0], in_sem.at[0]),
        pltpu.make_async_copy(q_hbm.at[:, half(1)], q.at[1], in_sem.at[1]),
        pltpu.make_async_copy(k_hbm, kb.at[0], in_sem.at[2]),
        pltpu.make_async_copy(okv_hbm.at[pl.ds(0, T)], ok, in_sem.at[3]),
        pltpu.make_async_copy(okv_hbm.at[pl.ds(T, T)], ov, in_sem.at[4]),
        pltpu.make_async_copy(len_hbm, len_ref, in_sem.at[5]),
        pltpu.make_async_copy(v_hbm, vb.at[0], in_sem.at[6]),
    ]
    for load in loads:
        load.start()
    barrier = pltpu.get_barrier_semaphore()
    for other in (left, right, up, down, far):
        pl.semaphore_signal(barrier, inc=1, device_id={"ctx": other}, device_id_type=MESH)

    def remote(src, dst, ssem, rsem, to):
        return pltpu.make_async_remote_copy(
            src_ref=src, dst_ref=dst, send_sem=ssem, recv_sem=rsem,
            device_id={"ctx": to}, device_id_type=MESH)

    def q_copy(n):
        dst, to = 2 + n, (right, left)[n % 2]
        src = q.at[n - 2 if n > 3 else (0, 1, 1, 0)[n]]
        return remote(src, q.at[dst], q_ssem.at[n], q_rsem.at[n], to)

    def ring_copy(n, buf, ssem, rsem):
        place, to = half(n % 2), (up, down)[n % 2]
        src = buf.at[1, place] if n > 3 else buf.at[0, half((0, 1, 1, 0)[n])]
        return remote(src, buf.at[1 + n // 2, place], ssem.at[n], rsem.at[n], to)

    def k_copy(n):
        return ring_copy(n, kb, k_ssem, k_rsem)

    def v_copy(n):
        return ring_copy(n, vb, v_ssem, v_rsem)

    def o_copy(n):
        to = (far, far, right, right, left, left)[n]
        return (remote(o_send.at[n], o_recv.at[n], o_ssem.at[n], o_rsem.at[n], to),
                remote(st_send.at[n], st_recv.at[n], st_ssem.at[n], st_rsem.at[n], to))

    def send_o(n, unit):
        o_send[n] = acc[unit].astype(BF16)
        for h in range(4):
            cols = slice(h * T, (h + 1) * T)
            st_send[n, h:h + 1, :] = mx[unit, 0:1, cols]
            st_send[n, 4 + h:5 + h, :] = sm[unit, 0:1, cols]
        for c in o_copy(n):
            c.start()

    def merge(unit, n):
        for c in o_copy(n):
            c.wait_recv()
        m, l = mx[unit, 0:1], sm[unit, 0:1]
        m2 = jnp.concatenate([st_recv[n, h:h + 1, :] for h in range(4)], axis=1)
        l2 = jnp.concatenate([st_recv[n, h:h + 1, :] for h in range(4, 8)], axis=1)
        new = jnp.maximum(m, m2)
        a, a2 = jnp.exp2((m - new) * SCALE), jnp.exp2((m2 - new) * SCALE)
        acc[unit] = acc[unit] * a + o_recv[n].astype(F32) * a2
        sm[unit, 0:1] = l * a + l2 * a2
        mx[unit, 0:1] = new

    def rows_of(unit, lo, hi):
        return jnp.concatenate([q[unit, :, h * D:(h + 1) * D] for h in range(lo, hi)], axis=0)

    def dot(a, b, da, db):
        return lax.dot_general(a, b, (((da,), (db,)), ((), ())), preferred_element_type=F32)

    def scores(i, u, s_ref, x_ref):
        slot, pair = block_of(i)
        cols = slice(u * PART, (u + 1) * PART)
        s = dot(kb[pair], rows_of(2 * slot + u // 2, 2 * (u % 2), 2 * (u % 2) + 2), 1, 1)
        s_ref[:, cols] = s
        x_ref[:, cols] = jnp.broadcast_to(jnp.max(s, axis=0, keepdims=True), (8, PART))

    def absorb(i, u, s_ref, x_ref):
        slot, pair = block_of(i)
        unit, cols = 2 * slot + u // 2, slice(u % 2 * PART, (u % 2 + 1) * PART)
        here = slice(u * PART, (u + 1) * PART)
        m, l = mx[unit, 0:1, cols], sm[unit, 0:1, cols]
        new = jnp.maximum(m, x_ref[0:1, here])
        p = jnp.exp2(s_ref[:, here] * SCALE - new * SCALE)
        a = jnp.exp2((m - new) * SCALE)
        d = dot(vb[pair], p.astype(BF16), 0, 0)
        sm[unit, 0:1, cols] = l * a + jnp.sum(p, axis=0, keepdims=True)
        acc[unit, :, cols] = acc[unit, :, cols] * a + d
        mx[unit, 0:1, cols] = new

    def block(i, cur, nxt):
        for u in range(4):
            if nxt is not None:
                scores(i + 1, u, *nxt)
            absorb(i, u, *cur)

    loads[0].wait()
    loads[1].wait()
    pl.semaphore_wait(barrier, 5)
    for n in range(4):
        q_copy(n).start()
    for n in range(2, 8):
        acc[n] = jnp.zeros((D, HALF), F32)
        mx[n, 0:1] = jnp.full((1, HALF), -1e30, F32)
        sm[n, 0:1] = jnp.zeros((1, HALF), F32)
    for n in range(2, 6):
        loads[n].wait()

    length = len_ref[0]
    key_at = lax.broadcasted_iota(jnp.int32, (T, HALF), 0)
    token = lax.rem(lax.broadcasted_iota(jnp.int32, (T, HALF), 1), T)
    visible = (key_at <= token) & (key_at < length)
    for n in range(2):
        s = jnp.where(visible, dot(ok[...], rows_of(n, 0, 4), 1, 1), -1e30)
        m = jnp.max(s, axis=0, keepdims=True)
        p = jnp.exp2(s * SCALE - m * SCALE)
        acc[n] = dot(ov[...], p.astype(BF16), 0, 0)
        mx[n, 0:1] = m
        sm[n, 0:1] = jnp.sum(p, axis=0, keepdims=True)
    for u in range(4):
        scores(0, u, s0, x0)
    loads[6].wait()

    even, odd = (s0, x0), (s1, x1)

    def receive(copy, *numbers):
        for n in numbers:
            copy(n).wait_recv()

    def q_needed(slot):
        if slot == 1:
            receive(q_copy, 0, 1)
            q_copy(4).start()
            q_copy(5).start()
        else:
            receive(q_copy, *((2, 3) if slot == 2 else (4, 5)))

    def ring_needed(copy, pair):
        receive(copy, 2 * pair - 2, 2 * pair - 1)
        if pair == 1:
            copy(4).start()
            copy(5).start()

    def send_slot(slot):
        for n, unit in (((2, 3), (4, 2)), ((3, 5), (5, 4)), ((0, 6), (1, 7)))[slot - 1]:
            send_o(n, unit)

    def before(i):
        todo = []
        if i > 0:
            done = ORDER[i - 1][0]
            if done > 0 and all(slot != done for slot, _ in ORDER[i:]):
                todo.append((send_slot, done))
        slot, pair = ORDER[i]
        if pair > 0 and all(p != pair for _, p in ORDER[:i]):
            todo.append((lambda p: ring_needed(v_copy, p), pair))
        if i + 1 < BLOCKS:
            slot, pair = ORDER[i + 1]
            if slot > 0 and all(t != slot for t, _ in ORDER[:i + 1]):
                todo.append((q_needed, slot))
            if pair > 0 and all(p != pair for _, p in ORDER[:i + 1]):
                todo.append((lambda p: ring_needed(k_copy, p), pair))
        return todo

    def body(j, carry):
        for parity, (cur, nxt) in enumerate(((odd, even), (even, odd))):
            for k in range(BLOCKS // 2 - 1):
                todo = before(1 + 2 * k + parity)
                if todo:
                    @pl.when(j == k)
                    def _():
                        for act, what in todo:
                            act(what)
            block(1 + 2 * j + parity, cur, nxt)
        return carry

    block(0, even, None)
    for n in range(4):
        k_copy(n).start()
        v_copy(n).start()
    for act, what in before(0):
        act(what)
    for u in range(4):
        scores(1, u, *odd)
    lax.fori_loop(0, BLOCKS // 2 - 1, body, 0)
    for act, what in before(BLOCKS - 1):
        act(what)
    block(BLOCKS - 1, odd, None)
    for unit, n in ((0, 0), (1, 1), (0, 4), (1, 2)):
        merge(unit, n)

    rows = lax.broadcasted_iota(jnp.int32, (T, D), 0)
    writes = []
    for unit, n in ((0, 3), (1, 5)):
        merge(unit, n)
        result = acc[unit] / sm[unit, 0:1]
        for h in range(4):
            piece = result[:, h * T:(h + 1) * T].T
            out[:, (unit * 4 + h) * D:(unit * 4 + h + 1) * D] = jnp.where(rows < length, piece, 0.0).astype(BF16)
        write = pltpu.make_async_copy(out.at[:, half(unit)], out_hbm.at[:, half(unit)], in_sem.at[7 + unit])
        write.start()
        writes.append(write)
    for write in writes:
        write.wait()

    for n in range(6):
        for c in (q_copy(n), k_copy(n), v_copy(n), *o_copy(n)):
            c.wait_send()


def shards(queries, prefix_keys, prefix_values, own_keys, own_values, lengths):
    dma = pltpu.SemaphoreType.DMA
    return pl.pallas_call(
        kernel,
        out_shape=jax.ShapeDtypeStruct((T, H * D), BF16),
        in_specs=[pl.BlockSpec(memory_space=pltpu.HBM)] * 5,
        out_specs=pl.BlockSpec(memory_space=pltpu.HBM),
        scratch_shapes=[
            pltpu.SMEM((1,), jnp.int32),
            pltpu.VMEM((T, H * D), BF16),
            pltpu.VMEM((8, T, HALF), BF16),
            pltpu.VMEM((4, ROWS, D), BF16),
            pltpu.VMEM((4, ROWS, D), BF16),
            pltpu.VMEM((T, D), BF16),
            pltpu.VMEM((T, D), BF16),
            pltpu.VMEM((8, D, HALF), F32),
            pltpu.VMEM((8, 8, HALF), F32),
            pltpu.VMEM((8, 8, HALF), F32),
            pltpu.VMEM((ROWS, 2 * HALF), F32),
            pltpu.VMEM((ROWS, 2 * HALF), F32),
            pltpu.VMEM((8, 2 * HALF), F32),
            pltpu.VMEM((8, 2 * HALF), F32),
            pltpu.VMEM((6, D, HALF), BF16),
            pltpu.VMEM((6, 8, T), F32),
            pltpu.VMEM((6, D, HALF), BF16),
            pltpu.VMEM((6, 8, T), F32),
        ] + [dma((9,))] + [dma((6,))] * 10,
        compiler_params=pltpu.CompilerParams(
            collective_id=0, has_side_effects=True, vmem_limit_bytes=5355 * 2**20 // 100),
        cost_estimate=pl.CostEstimate(flops=2**33, bytes_accessed=2**21, transcendentals=2**24),
    )(queries, prefix_keys, prefix_values, jnp.concatenate([own_keys, own_values], axis=0), lengths)


def solution(mesh):
    rows = P(("scene", "ctx"), "tp")
    return jax.shard_map(
        shards,
        mesh=mesh,
        in_specs=(rows, rows, rows, rows, rows, P(("scene", "ctx"))),
        out_specs=rows,
        check_vma=False,
    )
```

```python
import math

import jax
import jax.numpy as jnp
from jax import lax
from jax.experimental import pallas as pl
from jax.experimental.pallas import tpu as pltpu
from jax.sharding import PartitionSpec as P

MESH = pl.DeviceIdType.MESH
F32, BF16 = jnp.float32, jnp.bfloat16
D = 128
H = 8
T = 128
ROWS = 1024
HALF = 512
PART = 256
SIDE = 4
SCALE = math.log2(math.e) / math.sqrt(D)


ORDER = ((0, 0), (1, 0), (2, 0), (1, 1), (2, 1), (3, 0), (3, 1), (3, 2), (3, 3), (1, 2), (1, 3), (2, 2), (2, 3), (0, 1), (0, 2), (0, 3))
BLOCKS = len(ORDER)


def block_of(i):
    if isinstance(i, int):
        return ORDER[i]
    found = list(ORDER[0])
    for k in range(1, BLOCKS):
        reached = lax.div(i + (BLOCKS - k), BLOCKS)
        for part in range(2):
            step = ORDER[k][part] - ORDER[k - 1][part]
            if step:
                found[part] = found[part] + step * reached
    return found


def kernel(q_hbm, k_hbm, v_hbm, okv_hbm, len_hbm, out_hbm,
           len_ref, out, q, kb, vb, ok, ov, acc, mx, sm, s0, s1, x0, x1,
           o_send, st_send, o_recv, st_recv,
           in_sem, q_ssem, q_rsem, k_ssem, k_rsem, v_ssem, v_rsem, o_ssem, o_rsem, st_ssem, st_rsem):
    me = lax.axis_index("ctx")
    y, x = lax.div(me, SIDE), lax.rem(me, SIDE)
    turn = lax.axis_index("scene")

    def at(dx, dy):
        return lax.rem(y + dy, SIDE) * SIDE + lax.rem(x + dx, SIDE)

    right, left = at(1 - turn, turn), at((1 - turn) * 3, turn * 3)
    up, down = at(turn, 1 - turn), at(turn * 3, (1 - turn) * 3)
    far = at((1 - turn) * 2, turn * 2)

    def half(n):
        return pl.ds(n * HALF, HALF)

    loads = [
        pltpu.make_async_copy(q_hbm.at[:, half(0)], q.at[0], in_sem.at[0]),
        pltpu.make_async_copy(q_hbm.at[:, half(1)], q.at[1], in_sem.at[1]),
        pltpu.make_async_copy(k_hbm, kb.at[0], in_sem.at[2]),
        pltpu.make_async_copy(okv_hbm.at[pl.ds(0, T)], ok, in_sem.at[3]),
        pltpu.make_async_copy(okv_hbm.at[pl.ds(T, T)], ov, in_sem.at[4]),
        pltpu.make_async_copy(len_hbm, len_ref, in_sem.at[5]),
        pltpu.make_async_copy(v_hbm, vb.at[0], in_sem.at[6]),
    ]
    for load in loads:
        load.start()
    barrier = pltpu.get_barrier_semaphore()
    for other in (left, right, up, down, far):
        pl.semaphore_signal(barrier, inc=1, device_id={"ctx": other}, device_id_type=MESH)

    def remote(src, dst, ssem, rsem, to):
        return pltpu.make_async_remote_copy(
            src_ref=src, dst_ref=dst, send_sem=ssem, recv_sem=rsem,
            device_id={"ctx": to}, device_id_type=MESH)

    def q_copy(n):
        dst, to = 2 + n, (right, left)[n % 2]
        src = q.at[n - 2] if n > 3 else q_hbm.at[:, half((0, 1, 1, 0)[n])]
        return remote(src, q.at[dst], q_ssem.at[n], q_rsem.at[n], to)

    def ring_copy(n, hbm, buf, ssem, rsem):
        place, to = half(n % 2), (up, down)[n % 2]
        src = buf.at[1, place] if n > 3 else hbm.at[half((0, 1, 1, 0)[n])]
        return remote(src, buf.at[1 + n // 2, place], ssem.at[n], rsem.at[n], to)

    def k_copy(n):
        return ring_copy(n, k_hbm, kb, k_ssem, k_rsem)

    def v_copy(n):
        return ring_copy(n, v_hbm, vb, v_ssem, v_rsem)

    def o_copy(n):
        to = (far, far, right, right, left, left)[n]
        return (remote(o_send.at[n], o_recv.at[n], o_ssem.at[n], o_rsem.at[n], to),
                remote(st_send.at[n], st_recv.at[n], st_ssem.at[n], st_rsem.at[n], to))

    def send_o(n, unit):
        o_send[n] = acc[unit].astype(BF16)
        for h in range(4):
            cols = slice(h * T, (h + 1) * T)
            st_send[n, h:h + 1, :] = mx[unit, 0:1, cols]
            st_send[n, 4 + h:5 + h, :] = sm[unit, 0:1, cols]
        for c in o_copy(n):
            c.start()

    def merge(unit, n):
        for c in o_copy(n):
            c.wait_recv()
        m, l = mx[unit, 0:1], sm[unit, 0:1]
        m2 = jnp.concatenate([st_recv[n, h:h + 1, :] for h in range(4)], axis=1)
        l2 = jnp.concatenate([st_recv[n, h:h + 1, :] for h in range(4, 8)], axis=1)
        new = jnp.maximum(m, m2)
        a, a2 = jnp.exp2((m - new) * SCALE), jnp.exp2((m2 - new) * SCALE)
        acc[unit] = acc[unit] * a + o_recv[n].astype(F32) * a2
        sm[unit, 0:1] = l * a + l2 * a2
        mx[unit, 0:1] = new

    def rows_of(unit, lo, hi):
        return jnp.concatenate([q[unit, :, h * D:(h + 1) * D] for h in range(lo, hi)], axis=0)

    def dot(a, b, da, db):
        return lax.dot_general(a, b, (((da,), (db,)), ((), ())), preferred_element_type=F32)

    def scores(i, u, s_ref, x_ref):
        slot, pair = block_of(i)
        cols = slice(u * PART, (u + 1) * PART)
        s = dot(kb[pair], rows_of(2 * slot + u // 2, 2 * (u % 2), 2 * (u % 2) + 2), 1, 1)
        s_ref[:, cols] = s
        x_ref[:, cols] = jnp.broadcast_to(jnp.max(s, axis=0, keepdims=True), (8, PART))

    def absorb(i, u, s_ref, x_ref):
        slot, pair = block_of(i)
        unit, cols = 2 * slot + u // 2, slice(u % 2 * PART, (u % 2 + 1) * PART)
        here = slice(u * PART, (u + 1) * PART)
        m, l = mx[unit, 0:1, cols], sm[unit, 0:1, cols]
        new = jnp.maximum(m, x_ref[0:1, here])
        p = jnp.exp2(s_ref[:, here] * SCALE - new * SCALE)
        a = jnp.exp2((m - new) * SCALE)
        d = dot(vb[pair], p.astype(BF16), 0, 0)
        sm[unit, 0:1, cols] = l * a + jnp.sum(p, axis=0, keepdims=True)
        acc[unit, :, cols] = acc[unit, :, cols] * a + d
        mx[unit, 0:1, cols] = new

    def block(i, cur, nxt):
        for u in range(4):
            if nxt is not None:
                scores(i + 1, u, *nxt)
            absorb(i, u, *cur)

    pl.semaphore_wait(barrier, 5)
    for n in range(4):
        q_copy(n).start()
    for n in range(2, 8):
        acc[n] = jnp.zeros((D, HALF), F32)
        mx[n, 0:1] = jnp.full((1, HALF), -1e30, F32)
        sm[n, 0:1] = jnp.zeros((1, HALF), F32)
    for n in range(6):
        loads[n].wait()

    length = len_ref[0]
    key_at = lax.broadcasted_iota(jnp.int32, (T, HALF), 0)
    token = lax.rem(lax.broadcasted_iota(jnp.int32, (T, HALF), 1), T)
    visible = (key_at <= token) & (key_at < length)
    for n in range(2):
        s = jnp.where(visible, dot(ok[...], rows_of(n, 0, 4), 1, 1), -1e30)
        m = jnp.max(s, axis=0, keepdims=True)
        p = jnp.exp2(s * SCALE - m * SCALE)
        acc[n] = dot(ov[...], p.astype(BF16), 0, 0)
        mx[n, 0:1] = m
        sm[n, 0:1] = jnp.sum(p, axis=0, keepdims=True)
    for u in range(4):
        scores(0, u, s0, x0)
    loads[6].wait()

    even, odd = (s0, x0), (s1, x1)

    def receive(copy, *numbers):
        for n in numbers:
            copy(n).wait_recv()

    def q_needed(slot):
        if slot == 1:
            receive(q_copy, 0, 1)
            q_copy(4).start()
            q_copy(5).start()
        else:
            receive(q_copy, *((2, 3) if slot == 2 else (4, 5)))

    def ring_needed(copy, pair):
        receive(copy, 2 * pair - 2, 2 * pair - 1)
        if pair == 1:
            copy(4).start()
            copy(5).start()

    def send_slot(slot):
        for n, unit in (((2, 3), (4, 2)), ((3, 5), (5, 4)), ((0, 6), (1, 7)))[slot - 1]:
            send_o(n, unit)

    def before(i):
        todo = []
        if i > 0:
            done = ORDER[i - 1][0]
            if done > 0 and all(slot != done for slot, _ in ORDER[i:]):
                todo.append((send_slot, done))
        slot, pair = ORDER[i]
        if pair > 0 and all(p != pair for _, p in ORDER[:i]):
            todo.append((lambda p: ring_needed(v_copy, p), pair))
        if i + 1 < BLOCKS:
            slot, pair = ORDER[i + 1]
            if slot > 0 and all(t != slot for t, _ in ORDER[:i + 1]):
                todo.append((q_needed, slot))
            if pair > 0 and all(p != pair for _, p in ORDER[:i + 1]):
                todo.append((lambda p: ring_needed(k_copy, p), pair))
        return todo

    def body(j, carry):
        for parity, (cur, nxt) in enumerate(((odd, even), (even, odd))):
            for k in range(BLOCKS // 2 - 1):
                todo = before(1 + 2 * k + parity)
                if todo:
                    @pl.when(j == k)
                    def _():
                        for act, what in todo:
                            act(what)
            block(1 + 2 * j + parity, cur, nxt)
        return carry

    block(0, even, None)
    for n in range(4):
        k_copy(n).start()
        v_copy(n).start()
    for act, what in before(0):
        act(what)
    for u in range(4):
        scores(1, u, *odd)
    lax.fori_loop(0, BLOCKS // 2 - 1, body, 0)
    for act, what in before(BLOCKS - 1):
        act(what)
    block(BLOCKS - 1, odd, None)
    for unit, n in ((0, 0), (1, 1), (0, 4), (1, 2)):
        merge(unit, n)

    rows = lax.broadcasted_iota(jnp.int32, (T, D), 0)
    writes = []
    for unit, n in ((0, 3), (1, 5)):
        merge(unit, n)
        result = acc[unit] * (1.0 / sm[unit, 0:1])
        for h in range(4):
            piece = result[:, h * T:(h + 1) * T].T
            out[:, (unit * 4 + h) * D:(unit * 4 + h + 1) * D] = jnp.where(rows < length, piece, 0.0).astype(BF16)
        write = pltpu.make_async_copy(out.at[:, half(unit)], out_hbm.at[:, half(unit)], in_sem.at[7 + unit])
        write.start()
        writes.append(write)
    for write in writes:
        write.wait()

    for n in range(6):
        for c in (q_copy(n), k_copy(n), v_copy(n), *o_copy(n)):
            c.wait_send()


def shards(queries, prefix_keys, prefix_values, own_keys, own_values, lengths):
    dma = pltpu.SemaphoreType.DMA
    return pl.pallas_call(
        kernel,
        out_shape=jax.ShapeDtypeStruct((T, H * D), BF16),
        in_specs=[pl.BlockSpec(memory_space=pltpu.HBM)] * 5,
        out_specs=pl.BlockSpec(memory_space=pltpu.HBM),
        scratch_shapes=[
            pltpu.SMEM((1,), jnp.int32),
            pltpu.VMEM((T, H * D), BF16),
            pltpu.VMEM((8, T, HALF), BF16),
            pltpu.VMEM((4, ROWS, D), BF16),
            pltpu.VMEM((4, ROWS, D), BF16),
            pltpu.VMEM((T, D), BF16),
            pltpu.VMEM((T, D), BF16),
            pltpu.VMEM((8, D, HALF), F32),
            pltpu.VMEM((8, 8, HALF), F32),
            pltpu.VMEM((8, 8, HALF), F32),
            pltpu.VMEM((ROWS, 2 * HALF), F32),
            pltpu.VMEM((ROWS, 2 * HALF), F32),
            pltpu.VMEM((8, 2 * HALF), F32),
            pltpu.VMEM((8, 2 * HALF), F32),
            pltpu.VMEM((6, D, HALF), BF16),
            pltpu.VMEM((6, 8, T), F32),
            pltpu.VMEM((6, D, HALF), BF16),
            pltpu.VMEM((6, 8, T), F32),
        ] + [dma((9,))] + [dma((6,))] * 10,
        compiler_params=pltpu.CompilerParams(
            collective_id=0, has_side_effects=True, vmem_limit_bytes=5355 * 2**20 // 100),
        cost_estimate=pl.CostEstimate(flops=2**33, bytes_accessed=2**21, transcendentals=2**24),
    )(queries, prefix_keys, prefix_values, jnp.concatenate([own_keys, own_values], axis=0), lengths)


def solution(mesh):
    rows = P(("scene", "ctx"), "tp")
    return jax.shard_map(
        shards,
        mesh=mesh,
        in_specs=(rows, rows, rows, rows, rows, P(("scene", "ctx"))),
        out_specs=rows,
        check_vma=False,
    )
```
